128 devices in a mesh: tm: 32 (over x, y, core), expert: 4 (over z).
Axes of the slice: x: 4, y: 4, z: 4, core: 2. Of those that a mesh axis runs over, the one named last changes fastest.
Arguments:
- queries: bfloat16 [32768, 1536], P(('tm', 'expert')), may hold values from -300 to 300
- key_value: bfloat16 [2, 32768, 1536], P(None, ('tm', 'expert')), may hold values from -64 to 64
- conv_kernel: float32 [31, 1536], replicated, may hold values from -1 to 1
- conv_gain: float32 [1536], replicated, may hold values from 0.1 to 1.9
- ffn_gain: float32 [1536], replicated, may hold values from 0.1 to 1.9
- expert_gate: float32 [32768], P(('tm', 'expert')), may hold values from 0.5 to 2
- primary: int32 [32768], P(('tm', 'expert')), may hold values from 0 to 63, as said below
- secondary: int32 [32768], P(('tm', 'expert')), may hold values from 0 to 63, as said below
- overflow: int32 [32768], P(('tm', 'expert')), may hold values from 0 to 1
- slot: int32 [32768], P(('tm', 'expert')), may hold values from 0 to 5, as said below
- w_in: bfloat16 [64, 1536, 6144], P('tm', None, 'expert'), may hold values from -0.15625 to 0.15625
- w_out: bfloat16 [64, 6144, 1536], P('tm', 'expert'), may hold values from -0.078125 to 0.078125
Outputs:
- block_out: bfloat16 [32768, 1536], P(('tm', 'expert'))
The draws below stay inside these ranges and needn't reach their ends.
Inputs may be any that keep to these rules, and one draw needn't show every extreme that they name: `primary`: differs from secondary in every frame. `secondary`: differs from primary in every frame. Among the 256 frames of one device (aligned blocks), no two with the same serving expert share a slot; so at most 6 frames of one device go to one expert, and in every draw one expert receives exactly 6 frames from every device.
All inputs are finite; a program needn't handle non-finite values.
Results may differ from the reference program's by a relative error of at most 0.012.
Values may be sent and summed in bfloat16 or wider, within the bound.
No kernel may reach another device: no remote copies, remote signals or barrier semaphores. Data moves between devices by JAX's collectives and lax.ppermute only.
A program may use at most 128 MiB of HBM per device.

```python
import math
import jax
import jax.numpy as jnp
from jax import lax

D = 1536
HEADS = 24
FF = 6144
KERNEL = 31
HALF = 256
FR_DEV = 256
EXPERTS = 64
CAP = 6
FRAMES = 32768
N_EXPERT = 4


def route_table(key):
    devices_all = FRAMES // FR_DEV
    slot_total = EXPERTS * CAP
    hot_expert = jax.random.randint(jax.random.fold_in(key, 101), (), 0, EXPERTS)

    def one_device(device_key):
        scores = jax.random.randint(device_key, (slot_total,), 0, 1 << 16) * slot_total + jnp.arange(slot_total, dtype=jnp.int32)
        scores = jnp.where(jnp.arange(slot_total, dtype=jnp.int32) // CAP == hot_expert, scores + (1 << 29), scores)
        chosen = lax.top_k(scores, FR_DEV)[1]
        shuffle = jax.random.permutation(jax.random.fold_in(device_key, 1), FR_DEV)
        return chosen[shuffle]
    device_keys = jax.random.split(jax.random.fold_in(key, 102), devices_all)
    target = jax.vmap(one_device)(device_keys).reshape(FRAMES).astype(jnp.int32)
    served = target // CAP
    slot_ids = target % CAP
    spilled = (jax.random.randint(jax.random.fold_in(key, 103), (FRAMES,), 0, 4) == 0).astype(jnp.int32)
    other_expert = (served + 1 + jax.random.randint(jax.random.fold_in(key, 104), (FRAMES,), 0, EXPERTS - 1)) % EXPERTS
    first_pick = jnp.where(spilled == 1, other_expert, served)
    second = jnp.where(spilled == 1, served, other_expert)
    return (first_pick, second, spilled, slot_ids)


def draw_queries(key, part):
    key = jax.random.fold_in(key, 11)
    values = jnp.clip(jax.random.normal(key, (FRAMES, D), jnp.float32), -6.0, 6.0)
    return values.astype(jnp.bfloat16)


def draw_key_value(key, part):
    key = jax.random.fold_in(key, 12)
    values = jnp.clip(jax.random.normal(key, (2, FRAMES, D), jnp.float32), -6.0, 6.0)
    return values.astype(jnp.bfloat16)


def draw_primary(key, part):
    table = route_table(key)
    return table[0]


def draw_secondary(key, part):
    table = route_table(key)
    return table[1]


def draw_overflow(key, part):
    table = route_table(key)
    return table[2]


def draw_slot(key, part):
    table = route_table(key)
    return table[3]


def levels(own_key, shape, pieces, low, top_value):
    level, own = 1.0, jax.random.fold_in(own_key, 6)
    for dim, shards_of in pieces:
        heights = jnp.exp(jax.random.uniform(jax.random.fold_in(own, dim), (shards_of,), jnp.float32, low / len(pieces), top_value / len(pieces)))
        level = level * jnp.repeat(heights, shape[dim] // shards_of).reshape([-1 if axis == dim else 1 for axis in range(len(shape))])
    return level


def gaussian(stream_key, extent, width, most, cuts=(), kind=jnp.bfloat16):
    values = jax.random.normal(stream_key, extent, jnp.float32) * width
    if len(cuts) > 0:
        values = levels(stream_key, extent, cuts, -0.22, 0.18) * values
    return jnp.clip(values, min=-most, max=most).astype(kind)


def setup_inputs(seed: int = 0) -> dict:
    splits = jax.random.split(jax.random.key(seed), 13)
    queries = draw_queries(jax.random.fold_in(splits[12], 71), 0)
    key_value = draw_key_value(jax.random.fold_in(splits[12], 71), 0)
    conv_kernel = gaussian(splits[2], (KERNEL, D), KERNEL ** -0.5, 1.0, (), jnp.float32)
    conv_gain = jnp.clip(1.0 + 0.18 * jax.random.normal(splits[3], (D,), jnp.float32), 0.1, 1.9)
    ffn_gain = jnp.clip(1.0 + 0.18 * jax.random.normal(splits[4], (D,), jnp.float32), 0.1, 1.9)
    expert_gate = jnp.clip(jnp.exp(math.log(2.0) - 1.3862944 * jax.random.uniform(splits[5], (FRAMES,), jnp.float32) ** levels(splits[5], (FRAMES,), ((0, 128),), -0.2, 0.2)), 0.5, 2.0)
    primary = draw_primary(jax.random.fold_in(splits[12], 71), 0)
    secondary = draw_secondary(jax.random.fold_in(splits[12], 71), 0)
    overflow = draw_overflow(jax.random.fold_in(splits[12], 71), 0)
    slot = draw_slot(jax.random.fold_in(splits[12], 71), 0)
    w_in = gaussian(splits[10], (EXPERTS, D, FF), D ** -0.5, 0.15625, ((0, 32), (2, 4)))
    w_out = gaussian(splits[11], (EXPERTS, FF, D), FF ** -0.5, 0.078125, ((0, 32), (1, 4)))
    return dict(queries=queries, key_value=key_value, conv_kernel=conv_kernel, conv_gain=conv_gain, ffn_gain=ffn_gain, expert_gate=expert_gate, primary=primary, secondary=secondary, overflow=overflow, slot=slot, w_in=w_in, w_out=w_out)


def rms_scale(values, gain):
    return values * lax.rsqrt(lax.optimization_barrier(jnp.mean(values * values, axis=-1, keepdims=True)) + 1e-06) * gain

def attend(query_block, key_block, first_row, total_rows):
    block_rows, model_width = query_block.shape
    head_width = model_width // HEADS
    key_span = key_block.shape[1]
    query_heads = query_block.astype(jnp.float32).reshape(block_rows, HEADS, head_width)
    key_heads = key_block[0].astype(jnp.float32).reshape(key_span, HEADS, head_width)
    value_heads = key_block[1].astype(jnp.float32).reshape(key_span, HEADS, head_width)
    scores = jnp.einsum('qhd,khd->hqk', query_heads, key_heads) / math.sqrt(head_width)
    query_pos = first_row + jnp.arange(block_rows, dtype=jnp.int32)
    key_pos = first_row - HALF + jnp.arange(key_span, dtype=jnp.int32)
    allowed = (jnp.abs(query_pos[:, None] - key_pos[None, :]) < HALF) & (key_pos[None, :] >= 0) & (key_pos[None, :] < total_rows)
    scores = jnp.where(allowed[None], scores, -1e+30)
    highest = lax.optimization_barrier(jnp.max(scores, axis=-1, keepdims=True))
    expos = jnp.exp(scores - highest)
    probs = (expos / lax.optimization_barrier(jnp.sum(expos, axis=-1, keepdims=True))).astype(jnp.bfloat16)
    result = jnp.einsum('hqk,khd->qhd', probs.astype(jnp.float32), value_heads)
    return result.reshape(block_rows, model_width)

def reference(queries, key_value, conv_kernel, conv_gain, ffn_gain, expert_gate, primary, secondary, overflow, slot, w_in, w_out):
    blocks = FRAMES // FR_DEV
    padded_kv = jnp.pad(key_value, ((0, 0), (HALF, HALF), (0, 0)))

    def one_block(index):
        first_row = index * FR_DEV
        query_block = lax.dynamic_slice_in_dim(queries, first_row, FR_DEV, 0)
        key_block = lax.dynamic_slice_in_dim(padded_kv, first_row, FR_DEV + 2 * HALF, 1)
        return attend(query_block, key_block, first_row, FRAMES)
    attended = lax.map(one_block, jnp.arange(blocks, dtype=jnp.int32)).reshape(FRAMES, D)
    normed = rms_scale(attended, conv_gain).astype(jnp.bfloat16)
    reach = (KERNEL - 1) // 2
    padded = jnp.pad(normed, ((reach, reach), (0, 0)))
    conv_sum = jnp.zeros((FRAMES, D), jnp.float32)
    for offset in range(KERNEL):
        conv_sum = conv_sum + conv_kernel[offset] * padded[offset:offset + FRAMES].astype(jnp.float32)
    mixed = (normed.astype(jnp.float32) + jax.nn.silu(conv_sum)).astype(jnp.bfloat16)
    expert_in = rms_scale(mixed.astype(jnp.float32), ffn_gain).astype(jnp.bfloat16)
    served = jnp.where(overflow == 1, secondary, primary)
    device = jnp.arange(FRAMES, dtype=jnp.int32) // FR_DEV
    place = (device * CAP + slot) * EXPERTS + served
    dispatch = jnp.zeros((blocks * CAP * EXPERTS, D), jnp.bfloat16).at[place].set(expert_in)
    by_expert = jnp.moveaxis(dispatch.reshape(blocks * CAP, EXPERTS, D), 1, 0)
    quarter = FF // N_EXPERT

    def one_expert(operands):
        rows_in, first_weight, second_weight = operands
        hidden = jax.nn.silu(jnp.dot(rows_in, first_weight, preferred_element_type=jnp.float32)).astype(jnp.bfloat16)
        total = jnp.zeros((rows_in.shape[0], D), jnp.float32)
        for portion in range(N_EXPERT):
            partial_sum = jnp.dot(hidden[:, portion * quarter:(portion + 1) * quarter], second_weight[portion * quarter:(portion + 1) * quarter], preferred_element_type=jnp.float32).astype(jnp.bfloat16)
            total = total + lax.optimization_barrier(partial_sum).astype(jnp.float32)
        return total.astype(jnp.bfloat16)
    expert_out = lax.map(one_expert, (by_expert, w_in, w_out))
    picked = expert_out[served, device * CAP + slot]
    return (mixed.astype(jnp.float32) + expert_gate[:, None] * picked.astype(jnp.float32)).astype(jnp.bfloat16)
```

```python
import functools

import jax
import jax.numpy as jnp
from jax import lax
from jax.experimental import pallas as pl
from jax.experimental.pallas import tpu as pltpu
from jax.sharding import PartitionSpec as P

HEAD = 64
PAIR = 2 * HEAD
HALF = 256
TILE = 128
SPAN = 2 * HALF + TILE
EDGE = 16
GROUPS = (3, 3, 3, 3)
CHUNKS = 3
F32 = jnp.float32
BF16 = jnp.bfloat16


def call(body, out_shape, cost, **kw):
    flops, moved = cost
    return pl.pallas_call(
        body,
        out_shape=out_shape,
        cost_estimate=pl.CostEstimate(flops=flops, bytes_accessed=moved, transcendentals=0),
        compiler_params=pltpu.CompilerParams(vmem_limit_bytes=40 * 1024 * 1024),
        **kw,
    )


def attend_pair(edge_ref, q_ref, kv_ref, lo_ref, hi_ref, bias):
    @pl.when(pl.program_id(0) == 0)
    def _():
        row = lax.broadcasted_iota(jnp.int32, (TILE, SPAN), 0)
        col = lax.broadcasted_iota(jnp.int32, (TILE, SPAN), 1)
        for r in range(2):
            low = jnp.where(edge_ref[0] == 1, HALF - TILE * r, 0)
            high = jnp.where(edge_ref[1] == 1, 2 * HALF - TILE * r, SPAN)
            kept = (col > row) & (col - row < 2 * HALF) & (col >= low) & (col < high)
            bias[r] = jnp.where(kept, 0.0, -1e30)

    keys = jnp.concatenate([lo_ref[0], kv_ref[0], hi_ref[0]], axis=0)
    values = jnp.concatenate([lo_ref[1], kv_ref[1], hi_ref[1]], axis=0)
    q = q_ref[...]
    lane = lax.broadcasted_iota(jnp.int32, (1, PAIR), 1)
    first = lane < HEAD
    parts = [[], []]
    for h in range(2):
        mine = first if h == 0 else jnp.logical_not(first)
        qh = q * jnp.where(mine, 0.125, 0.0).astype(BF16)
        vh = values * jnp.where(mine, 1.0, 0.0).astype(BF16) + jnp.where(mine, 0.0, 1.0).astype(BF16)
        for r in range(2):
            rows = slice(r * TILE, r * TILE + TILE)
            span = slice(r * TILE, r * TILE + SPAN)
            s = lax.dot_general(
                qh[rows], keys[span], (((1,), (1,)), ((), ())), preferred_element_type=F32
            )
            s = s + bias[r]
            p = jnp.exp(s - jnp.max(s, axis=1, keepdims=True)).astype(BF16)
            parts[r].append(jnp.dot(p, vh[span], preferred_element_type=F32))
    halves = []
    for o0, o1 in parts:
        below = pltpu.roll(jnp.where(first, o1, o0), HEAD, 1)
        halves.append(jnp.where(first, o0, o1) / below)
    return halves


def attend_body(edge_ref, q_ref, kv_ref, lo_ref, hi_ref, out_ref, bias):
    for r, half in enumerate(attend_pair(edge_ref, q_ref, kv_ref, lo_ref, hi_ref, bias)):
        out_ref[r * TILE : (r + 1) * TILE] = half


def attend_norm_body(groups, edge_ref, q_ref, kv_ref, lo_ref, hi_ref, gain_ref, *rest):
    n = len(groups)
    earlier, (out_ref, low_ref, high_ref, bias, mine) = rest[:n], rest[n:]
    step = pl.program_id(0)
    for r, half in enumerate(attend_pair(edge_ref, q_ref, kv_ref, lo_ref, hi_ref, bias)):
        mine[step, r * TILE : (r + 1) * TILE] = half

    @pl.when(step == pl.num_programs(0) - 1)
    def _():
        blocks = [(ref, c) for ref, g in zip(earlier, groups) for c in range(g)]
        pieces = [(lambda ref=ref, c=c: ref[:, c * PAIR : (c + 1) * PAIR]) for ref, c in blocks]
        pieces += [(lambda c=c: mine[c]) for c in range(mine.shape[0])]
        total = jnp.zeros((2 * TILE, PAIR), F32)
        for piece in pieces:
            v = piece()
            total = total + v * v
        width = len(pieces) * PAIR
        scale = lax.rsqrt(jnp.sum(total, axis=1, keepdims=True) * (1.0 / width) + 1e-6)
        for c, piece in enumerate(pieces):
            cols = slice(c * PAIR, (c + 1) * PAIR)
            out_ref[:, cols] = (piece() * scale * gain_ref[:, cols]).astype(BF16)
        low_ref[...] = out_ref[:EDGE]
        high_ref[...] = out_ref[2 * TILE - EDGE :]


def attention(queries, key_value, low, high, edge, conv_gain):
    rows, width = queries.shape
    outs = []
    start = 0
    for g, pairs in enumerate(GROUPS):
        last = g == len(GROUPS) - 1
        base = [
            pl.BlockSpec(memory_space=pltpu.SMEM),
            pl.BlockSpec((rows, PAIR), lambda j, s=start: (0, s + j)),
            pl.BlockSpec((2, rows, PAIR), lambda j, s=start: (0, 0, s + j)),
            pl.BlockSpec((2, rows, PAIR), lambda j: (0, 0, j)),
            pl.BlockSpec((2, rows, PAIR), lambda j: (0, 0, j)),
        ]
        scratch = [pltpu.VMEM((2, TILE, SPAN), F32)]
        cost = (pairs * 16 * rows * SPAN * PAIR, pairs * 7 * rows * PAIR * 2)
        args = (edge, queries, key_value, low[g], high[g])
        if not last:
            outs.append(
                call(
                    attend_body,
                    jax.ShapeDtypeStruct((rows, pairs * PAIR), F32),
                    cost,
                    grid=(pairs,),
                    in_specs=base,
                    out_specs=pl.BlockSpec((rows, PAIR), lambda j: (0, j)),
                    scratch_shapes=scratch,
                )(*args)
            )
        else:
            whole = lambda *shape: pl.BlockSpec(shape, lambda j: (0,) * len(shape))
            return call(
                functools.partial(attend_norm_body, GROUPS[:-1]),
                [
                    jax.ShapeDtypeStruct((rows, width), BF16),
                    jax.ShapeDtypeStruct((EDGE, width), BF16),
                    jax.ShapeDtypeStruct((EDGE, width), BF16),
                ],
                cost,
                grid=(pairs,),
                in_specs=base + [whole(1, width)] + [whole(*o.shape) for o in outs],
                out_specs=[whole(rows, width), whole(EDGE, width), whole(EDGE, width)],
                scratch_shapes=scratch + [pltpu.VMEM((pairs, rows, PAIR), F32)],
            )(*args, conv_gain[None], *outs)
        start += pairs


def silu(v):
    return v / (1.0 + jnp.exp(-v))


def conv_rows(source, taps, first, count):
    total = jnp.zeros((count, PAIR), F32)
    for k in range(taps.shape[0]):
        total = total + taps[k : k + 1] * source[first + k : first + k + count]
    return source[first + 15 : first + 15 + count] + silu(total)


def inner_conv_body(normed_ref, taps_ref, out_ref, wide):
    wide[...] = normed_ref[...].astype(F32)
    count = 32
    for t in range(0, out_ref.shape[0], count):
        out_ref[t : t + count] = conv_rows(wide, taps_ref, EDGE + t - 15, count).astype(BF16)


def inner_conv(normed, taps):
    rows, width = normed.shape
    inner = rows - 2 * EDGE
    return call(
        inner_conv_body,
        jax.ShapeDtypeStruct((inner, width), BF16),
        (62 * inner * width * 64, 4 * rows * width),
        grid=(width // PAIR,),
        in_specs=[
            pl.BlockSpec((rows, PAIR), lambda j: (0, j)),
            pl.BlockSpec((taps.shape[0], PAIR), lambda j: (0, j)),
        ],
        out_specs=pl.BlockSpec((inner, PAIR), lambda j: (0, j)),
        scratch_shapes=[pltpu.VMEM((rows, PAIR), F32)],
    )(normed, taps)


def dispatch_body(normed_ref, inner_ref, low_ref, high_ref, taps_ref, gain_ref, place_ref, *rest):
    mixed_ref, outs, (wide,) = rest[0], rest[1:-1], rest[-1:]
    rows, width = normed_ref.shape
    for c in range(width // PAIR):
        cols = slice(c * PAIR, (c + 1) * PAIR)
        wide[0, :EDGE] = low_ref[:, cols].astype(F32)
        wide[0, EDGE:] = normed_ref[: 2 * EDGE, cols].astype(F32)
        wide[1, : 2 * EDGE] = normed_ref[rows - 2 * EDGE :, cols].astype(F32)
        wide[1, 2 * EDGE :] = high_ref[:, cols].astype(F32)
        taps = taps_ref.at[:, cols]
        mixed_ref[:EDGE, cols] = conv_rows(wide.at[0], taps, 1, EDGE).astype(BF16)
        mixed_ref[rows - EDGE :, cols] = conv_rows(wide.at[1], taps, 1, EDGE).astype(BF16)
    mixed_ref[EDGE : rows - EDGE] = inner_ref[...]
    mixed = mixed_ref[...].astype(F32)
    scale = lax.rsqrt(jnp.mean(mixed * mixed, axis=1, keepdims=True) + 1e-6)
    expert_in = (mixed * scale * gain_ref[...]).astype(BF16)
    first = 0
    for out_ref in outs:
        count = out_ref.shape[0]
        place = first + lax.broadcasted_iota(jnp.int32, (count, rows), 0)
        pick = jnp.where(place == place_ref[...], 1.0, 0.0).astype(BF16)
        out_ref[...] = jnp.dot(pick, expert_in, preferred_element_type=F32).astype(BF16)
        first += count


def dispatch(normed, inner, low, high, taps, gain, place, count):
    rows, width = normed.shape
    return call(
        dispatch_body,
        [jax.ShapeDtypeStruct((rows, width), BF16)]
        + [jax.ShapeDtypeStruct((count, width), BF16)] * CHUNKS,
        (2 * CHUNKS * count * rows * width, 8 * rows * width),
        scratch_shapes=[pltpu.VMEM((2, 3 * EDGE, PAIR), F32)],
    )(normed, inner, low, high, taps, gain[None], place[None])


def combine_body(mixed_ref, gate_ref, place_ref, *rest):
    parts, out_ref = rest[:-1], rest[-1]
    rows = mixed_ref.shape[0]
    total = None
    first = 0
    for part in parts:
        count = part.shape[0]
        place = first + lax.broadcasted_iota(jnp.int32, (rows, count), 1)
        pick = jnp.where(place == place_ref[...], 1.0, 0.0).astype(BF16)
        got = jnp.dot(pick, part[...], preferred_element_type=F32)
        total = got if total is None else total + got
        first += count
    out_ref[...] = (mixed_ref[...].astype(F32) + gate_ref[...] * total).astype(BF16)


def combine(mixed, gate, place, parts):
    rows, width = mixed.shape
    block = 256
    column = lambda n: pl.BlockSpec((n, block), lambda j: (0, j))
    fixed = pl.BlockSpec((rows, 1), lambda j: (0, 0))
    return call(
        combine_body,
        jax.ShapeDtypeStruct((rows, width), BF16),
        (2 * sum(p.shape[0] for p in parts) * rows * width, 8 * rows * width),
        grid=(width // block,),
        in_specs=[column(rows), fixed, fixed] + [column(p.shape[0]) for p in parts],
        out_specs=column(rows),
    )(mixed, gate[:, None], place[:, None], *parts)


def ffn_body(own, left, right, far0, far1, w_in, w_out, keep, up, down, up2, down2, rows_in, total):
    e, f = pl.program_id(0), pl.program_id(1)
    n = own.shape[1]

    @pl.when(f == 0)
    def _():
        rows_in[:n] = own[0]
        rows_in[n : 2 * n] = left[0]
        rows_in[2 * n : 3 * n] = right[0]

    @pl.when((f == 0) & (e == 0))
    def _():
        rows_in[3 * n :] = far0[...]

    @pl.when((f == 0) & (e == 1))
    def _():
        rows_in[3 * n :] = far1[...]

    hidden = silu(jnp.dot(rows_in[...], w_in[0], preferred_element_type=F32)).astype(BF16)
    part = jnp.dot(hidden, w_out[0], preferred_element_type=F32)

    @pl.when(f == 0)
    def _():
        total[...] = part

    @pl.when(f > 0)
    def _():
        total[...] += part

    done = f == pl.num_programs(1) - 1

    @pl.when(done)
    def _():
        keep[0] = total[:n].astype(BF16)

    @pl.when(done & (e == 0))
    def _():
        down[1] = total[n : 2 * n].astype(BF16)
        up2[...] = total[2 * n : 3 * n].astype(BF16)
        up[0] = total[3 * n :].astype(BF16)

    @pl.when(done & (e == 1))
    def _():
        down2[...] = total[n : 2 * n].astype(BF16)
        up[1] = total[2 * n : 3 * n].astype(BF16)
        down[0] = total[3 * n :].astype(BF16)


def ffn(own, left, right, far0, far1, w_in, w_out):
    experts, n, width = own.shape
    units = w_in.shape[2]
    step = 512
    each = pl.BlockSpec((1, n, width), lambda e, f: (e, 0, 0))
    both = pl.BlockSpec((2, n, width), lambda e, f: (0, 0, 0))
    one = pl.BlockSpec((n, width), lambda e, f: (0, 0))
    pair = jax.ShapeDtypeStruct((2, n, width), BF16)
    single = jax.ShapeDtypeStruct((n, width), BF16)
    return call(
        ffn_body,
        [pair, pair, pair, single, single],
        (experts * 4 * n * width * units * 4, 2 * experts * width * units * 2),
        grid=(experts, units // step),
        in_specs=[
            each,
            each,
            each,
            one,
            one,
            pl.BlockSpec((1, width, step), lambda e, f: (e, 0, f)),
            pl.BlockSpec((1, step, width), lambda e, f: (e, f, 0)),
        ],
        out_specs=[each, both, both, one, one],
        scratch_shapes=[pltpu.VMEM((4 * n, width), BF16), pltpu.VMEM((4 * n, width), F32)],
    )(own, left, right, far0, far1, w_in, w_out)


def on_device(
    queries,
    key_value,
    conv_kernel,
    conv_gain,
    ffn_gain,
    expert_gate,
    primary,
    secondary,
    overflow,
    slot,
    w_in,
    w_out,
):
    frame_rows, width = queries.shape
    time_count = lax.axis_size("tm")
    group_count = lax.axis_size("expert")
    devices = time_count * group_count
    index = lax.axis_index("tm") * group_count + lax.axis_index("expert")
    edge = jnp.stack([index == 0, index == devices - 1]).astype(jnp.int32)
    order = ("tm", "expert")
    onward = [(i, i + 1) for i in range(devices - 1)]
    back = [(i + 1, i) for i in range(devices - 1)]

    low, high = [], []
    start = 0
    for pairs in GROUPS:
        part = lax.slice_in_dim(key_value, start * PAIR, (start + pairs) * PAIR, axis=2)
        low.append(lax.ppermute(part, order, onward))
        high.append(lax.ppermute(part, order, back))
        start += pairs
    normed, first_rows, last_rows = attention(queries, key_value, low, high, edge, conv_gain)

    before = lax.ppermute(last_rows, order, onward)
    after = lax.ppermute(first_rows, order, back)
    inner = inner_conv(normed, conv_kernel)

    local = w_in.shape[0]
    experts = local * time_count
    slots = max(2, 3 * frame_rows // (2 * experts)) // CHUNKS
    count = experts * slots
    served = jnp.where(overflow == 1, secondary, primary)
    place = (slot // slots) * count + served * slots + slot % slots
    mixed, *chunks = dispatch(
        normed, inner, before, after, conv_kernel, ffn_gain, place, count
    )

    up = [(i, (i + 1) % group_count) for i in range(group_count)]
    down = [((i + 1) % group_count, i) for i in range(group_count)]
    returned = []
    for chunk in chunks:
        sent = chunk.reshape(time_count, local * slots, width)
        own = lax.all_to_all(sent, "tm", split_axis=0, concat_axis=0, tiled=True)
        own = own.reshape(time_count, local, slots, width).transpose(1, 0, 2, 3)
        own = own.reshape(local, time_count * slots, width)
        left = lax.ppermute(own, "expert", up)
        right = lax.ppermute(own, "expert", down)
        far0 = lax.ppermute(left[0], "expert", up)
        far1 = lax.ppermute(right[1], "expert", down)
        keep, go_up, go_down, up2, down2 = ffn(own, left, right, far0, far1, w_in, w_out)
        from_below = lax.ppermute(go_up, "expert", up)
        from_above = lax.ppermute(go_down, "expert", down)
        add = lambda *vs: sum(v.astype(F32) for v in vs).astype(BF16)
        up3 = lax.ppermute(add(up2, from_below[0]), "expert", up)
        down3 = lax.ppermute(add(down2, from_above[0]), "expert", down)
        summed = jnp.stack(
            [add(keep[0], from_above[1], up3), add(keep[1], from_below[1], down3)]
        )
        summed = summed.reshape(local, time_count, slots, width).transpose(1, 0, 2, 3)
        summed = summed.reshape(time_count, local * slots, width)
        got = lax.all_to_all(summed, "tm", split_axis=0, concat_axis=0, tiled=True)
        returned.append(got.reshape(count, width))
    return combine(mixed, expert_gate, place, returned)


def solution(mesh):
    in_specs = (
        P(("tm", "expert"), None),
        P(None, ("tm", "expert"), None),
        P(),
        P(),
        P(),
        P(("tm", "expert")),
        P(("tm", "expert")),
        P(("tm", "expert")),
        P(("tm", "expert")),
        P(("tm", "expert")),
        P("tm", None, "expert"),
        P("tm", "expert", None),
    )
    out_specs = P(("tm", "expert"), None)
    return jax.shard_map(
        on_device, mesh=mesh, in_specs=in_specs, out_specs=out_specs, check_vma=False
    )
```

```python
import functools

import jax
import jax.numpy as jnp
from jax import lax
from jax.experimental import pallas as pl
from jax.experimental.pallas import tpu as pltpu
from jax.sharding import PartitionSpec as P

HEAD = 64
PAIR = 2 * HEAD
HALF = 256
TILE = 128
SPAN = 2 * HALF + TILE
EDGE = 16
GROUPS = (6, 4, 2)
MIB = 1024 * 1024
STEP = 512
F32 = jnp.float32
BF16 = jnp.bfloat16


def call(body, out_shape, cost, vmem, **kw):
    flops, moved = cost
    return pl.pallas_call(
        body,
        out_shape=out_shape,
        cost_estimate=pl.CostEstimate(flops=flops, bytes_accessed=moved, transcendentals=0),
        compiler_params=pltpu.CompilerParams(vmem_limit_bytes=vmem * MIB),
        **kw,
    )


def attend_pair(edge_ref, q_ref, kv_ref, lo_ref, hi_ref, bias):
    @pl.when(pl.program_id(0) == 0)
    def _():
        row = lax.broadcasted_iota(jnp.int32, (TILE, SPAN), 0)
        col = lax.broadcasted_iota(jnp.int32, (TILE, SPAN), 1)
        for r in range(2):
            low = jnp.where(edge_ref[0] == 1, HALF - TILE * r, 0)
            high = jnp.where(edge_ref[1] == 1, 2 * HALF - TILE * r, SPAN)
            kept = (col > row) & (col - row < 2 * HALF) & (col >= low) & (col < high)
            bias[r] = jnp.where(kept, 0.0, -1e30)

    lane = lax.broadcasted_iota(jnp.int32, (1, PAIR), 1)
    first = lane < HEAD
    only0 = jnp.where(first, 0.125, 0.0).astype(BF16)
    only1 = jnp.where(first, 0.0, 0.125).astype(BF16)
    ones = jnp.ones((SPAN, PAIR), BF16)
    halves = []
    for r in range(2):
        if r == 0:
            join = lambda i: [lo_ref[i], kv_ref[i], hi_ref[i, :TILE]]
        else:
            join = lambda i: [lo_ref[i, TILE:], kv_ref[i], hi_ref[i]]
        q = q_ref[r * TILE : (r + 1) * TILE]
        both = jnp.concatenate([q * only0, q * only1], axis=0)
        s = lax.dot_general(
            both, jnp.concatenate(join(0), axis=0), (((1,), (1,)), ((), ())), preferred_element_type=F32
        )
        s = s + jnp.concatenate([bias[r], bias[r]], axis=0)
        p = jnp.exp(s - jnp.max(s, axis=1, keepdims=True)).astype(BF16)
        values = jnp.concatenate([jnp.concatenate(join(1), axis=0), ones], axis=1)
        o = jnp.dot(p, values, preferred_element_type=F32)
        o = o[:, :PAIR] / o[:, PAIR:]
        halves.append(jnp.where(first, o[:TILE], o[TILE:]))
    return halves


def attend_body(edge_ref, q_ref, kv_ref, lo_ref, hi_ref, out_ref, bias):
    for r, half in enumerate(attend_pair(edge_ref, q_ref, kv_ref, lo_ref, hi_ref, bias)):
        out_ref[r * TILE : (r + 1) * TILE] = half


def attend_norm_body(groups, edge_ref, q_ref, kv_ref, lo_ref, hi_ref, gain_ref, *rest):
    n = len(groups)
    earlier, (out_ref, low_ref, high_ref, bias, mine) = rest[:n], rest[n:]
    step = pl.program_id(0)
    for r, half in enumerate(attend_pair(edge_ref, q_ref, kv_ref, lo_ref, hi_ref, bias)):
        mine[step, r * TILE : (r + 1) * TILE] = half

    @pl.when(step == pl.num_programs(0) - 1)
    def _():
        blocks = [(ref, c) for ref, g in zip(earlier, groups) for c in range(g)]
        pieces = [(lambda ref=ref, c=c: ref[:, c * PAIR : (c + 1) * PAIR]) for ref, c in blocks]
        pieces += [(lambda c=c: mine[c]) for c in range(mine.shape[0])]
        total = jnp.zeros((2 * TILE, PAIR), F32)
        for piece in pieces:
            v = piece()
            total = total + v * v
        width = len(pieces) * PAIR
        scale = lax.rsqrt(jnp.sum(total, axis=1, keepdims=True) * (1.0 / width) + 1e-6)
        for c, piece in enumerate(pieces):
            cols = slice(c * PAIR, (c + 1) * PAIR)
            out_ref[:, cols] = (piece() * scale * gain_ref[:, cols]).astype(BF16)
        low_ref[...] = out_ref[:EDGE]
        high_ref[...] = out_ref[2 * TILE - EDGE :]


def attention(queries, key_value, low, high, edge, conv_gain):
    rows, width = queries.shape
    outs = []
    start = 0
    for g, pairs in enumerate(GROUPS):
        last = g == len(GROUPS) - 1
        base = [
            pl.BlockSpec(memory_space=pltpu.SMEM),
            pl.BlockSpec((rows, PAIR), lambda j, s=start: (0, s + j)),
            pl.BlockSpec((2, rows, PAIR), lambda j, s=start: (0, 0, s + j)),
            pl.BlockSpec((2, rows, PAIR), lambda j: (0, 0, j)),
            pl.BlockSpec((2, rows, PAIR), lambda j: (0, 0, j)),
        ]
        scratch = [pltpu.VMEM((2, TILE, SPAN), F32)]
        cost = (pairs * 16 * rows * SPAN * PAIR, pairs * 7 * rows * PAIR * 2)
        before, after = low[g], high[g]
        if outs:
            before, after, _ = lax.optimization_barrier((before, after, outs[-1]))
        args = (edge, queries, key_value, before, after)
        if not last:
            outs.append(
                call(
                    attend_body,
                    jax.ShapeDtypeStruct((rows, pairs * PAIR), F32),
                    cost,
                    16,
                    grid=(pairs,),
                    in_specs=base,
                    out_specs=pl.BlockSpec((rows, PAIR), lambda j: (0, j)),
                    scratch_shapes=scratch,
                )(*args)
            )
        else:
            whole = lambda *shape: pl.BlockSpec(shape, lambda j: (0,) * len(shape))
            return call(
                functools.partial(attend_norm_body, GROUPS[:-1]),
                [
                    jax.ShapeDtypeStruct((rows, width), BF16),
                    jax.ShapeDtypeStruct((EDGE, width), BF16),
                    jax.ShapeDtypeStruct((EDGE, width), BF16),
                ],
                cost,
                20,
                grid=(pairs,),
                in_specs=base + [whole(1, width)] + [whole(*o.shape) for o in outs],
                out_specs=[whole(rows, width), whole(EDGE, width), whole(EDGE, width)],
                scratch_shapes=scratch + [pltpu.VMEM((pairs, rows, PAIR), F32)],
            )(*args, conv_gain[None], *outs)
        start += pairs


def silu(v):
    half = 0.5 * v
    return half + half * jnp.tanh(half)


def conv_rows(source, taps, first, count):
    total = jnp.zeros((count, PAIR), F32)
    for k in range(taps.shape[0]):
        total = total + taps[k : k + 1] * source[first + k : first + k + count]
    return source[first + 15 : first + 15 + count] + silu(total)


def inner_conv_body(normed_ref, taps_ref, out_ref, wide):
    wide[...] = normed_ref[...].astype(F32)
    count = 32
    for t in range(0, out_ref.shape[0], count):
        out_ref[t : t + count] = conv_rows(wide, taps_ref, EDGE + t - 15, count).astype(BF16)


def inner_conv(normed, taps):
    rows, width = normed.shape
    inner = rows - 2 * EDGE
    return call(
        inner_conv_body,
        jax.ShapeDtypeStruct((inner, width), BF16),
        (62 * inner * width * 64, 4 * rows * width),
        16,
        grid=(width // PAIR,),
        in_specs=[
            pl.BlockSpec((rows, PAIR), lambda j: (0, j)),
            pl.BlockSpec((taps.shape[0], PAIR), lambda j: (0, j)),
        ],
        out_specs=pl.BlockSpec((inner, PAIR), lambda j: (0, j)),
        scratch_shapes=[pltpu.VMEM((rows, PAIR), F32)],
    )(normed, taps)


def dispatch_body(normed_ref, inner_ref, low_ref, high_ref, taps_ref, gain_ref, place_ref, *rest):
    mixed_ref, outs, (wide,) = rest[0], rest[1:-1], rest[-1:]
    rows, width = normed_ref.shape
    for c in range(width // PAIR):
        cols = slice(c * PAIR, (c + 1) * PAIR)
        wide[0, :EDGE] = low_ref[:, cols].astype(F32)
        wide[0, EDGE:] = normed_ref[: 2 * EDGE, cols].astype(F32)
        wide[1, : 2 * EDGE] = normed_ref[rows - 2 * EDGE :, cols].astype(F32)
        wide[1, 2 * EDGE :] = high_ref[:, cols].astype(F32)
        taps = taps_ref.at[:, cols]
        mixed_ref[:EDGE, cols] = conv_rows(wide.at[0], taps, 1, EDGE).astype(BF16)
        mixed_ref[rows - EDGE :, cols] = conv_rows(wide.at[1], taps, 1, EDGE).astype(BF16)
    mixed_ref[EDGE : rows - EDGE] = inner_ref[...]
    mixed = mixed_ref[...].astype(F32)
    scale = lax.rsqrt(jnp.mean(mixed * mixed, axis=1, keepdims=True) + 1e-6)
    expert_in = (mixed * scale * gain_ref[...]).astype(BF16)
    first = 0
    for out_ref in outs:
        count = out_ref.shape[0]
        place = first + lax.broadcasted_iota(jnp.int32, (count, rows), 0)
        pick = jnp.where(place == place_ref[...], 1.0, 0.0).astype(BF16)
        out_ref[...] = jnp.dot(pick, expert_in, preferred_element_type=F32).astype(BF16)
        first += count


def dispatch(normed, inner, low, high, taps, gain, place, counts):
    rows, width = normed.shape
    return call(
        dispatch_body,
        [jax.ShapeDtypeStruct((rows, width), BF16)]
        + [jax.ShapeDtypeStruct((count, width), BF16) for count in counts],
        (2 * sum(counts) * rows * width, 8 * rows * width),
        24,
        scratch_shapes=[pltpu.VMEM((2, 3 * EDGE, PAIR), F32)],
    )(normed, inner, low, high, taps, gain[None], place[None])


def combine_body(mixed_ref, gate_ref, place_ref, *rest):
    parts, out_ref = rest[:-1], rest[-1]
    rows = mixed_ref.shape[0]
    total = None
    first = 0
    for part in parts:
        count = part.shape[0]
        place = first + lax.broadcasted_iota(jnp.int32, (rows, count), 1)
        pick = jnp.where(place == place_ref[...], 1.0, 0.0).astype(BF16)
        got = jnp.dot(pick, part[...], preferred_element_type=F32)
        total = got if total is None else total + got
        first += count
    out_ref[...] = (mixed_ref[...].astype(F32) + gate_ref[...] * total).astype(BF16)


def combine(mixed, gate, place, parts):
    rows, width = mixed.shape
    block = 256
    column = lambda n: pl.BlockSpec((n, block), lambda j: (0, j))
    fixed = pl.BlockSpec((rows, 1), lambda j: (0, 0))
    return call(
        combine_body,
        jax.ShapeDtypeStruct((rows, width), BF16),
        (2 * sum(p.shape[0] for p in parts) * rows * width, 8 * rows * width),
        16,
        grid=(width // block,),
        in_specs=[column(rows), fixed, fixed] + [column(p.shape[0]) for p in parts],
        out_specs=column(rows),
    )(mixed, gate[:, None], place[:, None], *parts)


def ffn_body(own, left, right, far0, far1, w_in, w_out, keep, up, down, up2, down2, *scratch):
    rows_in, hidden, first, second, sems = scratch
    n, width = own.shape[1:]
    units = hidden.shape[1]
    step = STEP
    copies = {}
    for e in range(2):
        for which, (weight, held) in enumerate(((w_in, first), (w_out, second))):
            for t in range(weight.shape[2] // step):
                cols = slice(t * step, (t + 1) * step)
                copies[e, which, t] = pltpu.make_async_copy(
                    weight.at[e, :, cols], held.at[e, t], sems.at[e, which, t]
                )
                copies[e, which, t].start()
    for e in range(2):
        rows_in[:n] = own[e]
        rows_in[n : 2 * n] = left[e]
        rows_in[2 * n : 3 * n] = right[e]
        rows_in[3 * n :] = (far0 if e == 0 else far1)[...]
        for t in range(units // step):
            copies[e, 0, t].wait()
            part = jnp.dot(rows_in[...], first[e, t], preferred_element_type=F32)
            hidden[:, t * step : (t + 1) * step] = silu(part).astype(BF16)
        for t in range(width // step):
            copies[e, 1, t].wait()
            cols = slice(t * step, (t + 1) * step)
            part = jnp.dot(hidden[...], second[e, t], preferred_element_type=F32).astype(BF16)
            keep[e, :, cols] = part[:n]
            if e == 0:
                down[1, :, cols] = part[n : 2 * n]
                up2[:, cols] = part[2 * n : 3 * n]
                up[0, :, cols] = part[3 * n :]
            else:
                down2[:, cols] = part[n : 2 * n]
                up[1, :, cols] = part[2 * n : 3 * n]
                down[0, :, cols] = part[3 * n :]


def ffn(own, left, right, far0, far1, w_in, w_out):
    experts, n, width = own.shape
    units = w_in.shape[2]
    pair = jax.ShapeDtypeStruct((2, n, width), BF16)
    single = jax.ShapeDtypeStruct((n, width), BF16)
    return call(
        ffn_body,
        [pair, pair, pair, single, single],
        (experts * 4 * n * width * units * 4, 2 * experts * width * units * 2),
        50,
        in_specs=[pl.BlockSpec(memory_space=pltpu.VMEM)] * 5 + [pl.BlockSpec(memory_space=pl.ANY)] * 2,
        scratch_shapes=[
            pltpu.VMEM((4 * n, width), BF16),
            pltpu.VMEM((4 * n, units), BF16),
            pltpu.VMEM((2, units // STEP, width, STEP), BF16),
            pltpu.VMEM((2, width // STEP, units, STEP), BF16),
            pltpu.SemaphoreType.DMA((2, 2, max(units, width) // STEP)),
        ],
    )(own, left, right, far0, far1, w_in, w_out)


def on_device(
    queries,
    key_value,
    conv_kernel,
    conv_gain,
    ffn_gain,
    expert_gate,
    primary,
    secondary,
    overflow,
    slot,
    w_in,
    w_out,
):
    frame_rows, width = queries.shape
    time_count = lax.axis_size("tm")
    group_count = lax.axis_size("expert")
    devices = time_count * group_count
    index = lax.axis_index("tm") * group_count + lax.axis_index("expert")
    edge = jnp.stack([index == 0, index == devices - 1]).astype(jnp.int32)
    order = ("tm", "expert")
    onward = [(i, i + 1) for i in range(devices - 1)]
    back = [(i + 1, i) for i in range(devices - 1)]

    low, high = [], []
    start = 0
    source = key_value
    for pairs in GROUPS:
        part = lax.slice_in_dim(source, start * PAIR, (start + pairs) * PAIR, axis=2)
        low.append(lax.ppermute(part, order, onward))
        high.append(lax.ppermute(part, order, back))
        start += pairs
        source, _ = lax.optimization_barrier((key_value, part))
    normed, first_rows, last_rows = attention(queries, key_value, low, high, edge, conv_gain)

    before = lax.ppermute(last_rows, order, onward)
    after = lax.ppermute(first_rows, order, back)
    inner = inner_conv(normed, conv_kernel)

    local = w_in.shape[0]
    experts = local * time_count
    slots = max(2, 3 * frame_rows // (2 * experts))
    early = 2 * slots // 3
    sizes = (early, slots - early)
    served = jnp.where(overflow == 1, secondary, primary)
    place = jnp.where(
        slot < early,
        served * early + slot,
        experts * early + served * (slots - early) + slot - early,
    )
    mixed, *chunks = dispatch(
        normed, inner, before, after, conv_kernel, ffn_gain, place, [experts * c for c in sizes]
    )

    up = [(i, (i + 1) % group_count) for i in range(group_count)]
    down = [((i + 1) % group_count, i) for i in range(group_count)]
    add = lambda *vs: sum(v.astype(F32) for v in vs).astype(BF16)

    def arrive(chunk, size):
        sent = chunk.reshape(time_count, local * size, width)
        own = lax.all_to_all(sent, "tm", split_axis=0, concat_axis=0, tiled=True)
        own = own.reshape(time_count, local, size, width).transpose(1, 0, 2, 3)
        return own.reshape(local, time_count * size, width)

    def near(own):
        return lax.ppermute(own, "expert", up), lax.ppermute(own, "expert", down)

    def far(left, right):
        return lax.ppermute(left[0], "expert", up), lax.ppermute(right[1], "expert", down)

    def leave(summed, size):
        summed = summed.reshape(local, time_count, size, width).transpose(1, 0, 2, 3)
        summed = summed.reshape(time_count, local * size, width)
        got = lax.all_to_all(summed, "tm", split_axis=0, concat_axis=0, tiled=True)
        return got.reshape(experts * size, width)

    after = lambda values, *others: lax.optimization_barrier((tuple(values), others))[0]
    own_a = arrive(chunks[0], sizes[0])
    left_a, right_a = near(own_a)
    own_b = arrive(chunks[1], sizes[1])
    left_a, right_a = after((left_a, right_a), own_b)
    far_a = far(left_a, right_a)
    left_b, right_b = near(own_b)
    keep_a, go_up_a, go_down_a, up2_a, down2_a = ffn(own_a, left_a, right_a, *far_a, w_in, w_out)
    below_a, above_a = lax.ppermute(go_up_a, "expert", up), lax.ppermute(go_down_a, "expert", down)
    left_b, right_b = after((left_b, right_b), keep_a)
    far_b = far(left_b, right_b)
    up2_a, down2_a = add(up2_a, below_a[0]), add(down2_a, above_a[0])
    up3_a, down3_a = lax.ppermute(up2_a, "expert", up), lax.ppermute(down2_a, "expert", down)
    (own_b,) = after((own_b,), up2_a, down2_a)
    keep_b, go_up_b, go_down_b, up2_b, down2_b = ffn(own_b, left_b, right_b, *far_b, w_in, w_out)
    go_up_b, go_down_b = after((go_up_b, go_down_b), up3_a, down3_a)
    below_b, above_b = lax.ppermute(go_up_b, "expert", up), lax.ppermute(go_down_b, "expert", down)
    total_a = jnp.stack([add(keep_a[0], above_a[1], up3_a), add(keep_a[1], below_a[1], down3_a)])
    back_a = leave(total_a, sizes[0])
    below_b, above_b = after((below_b, above_b), total_a)
    up3_b = lax.ppermute(add(up2_b, below_b[0]), "expert", up)
    down3_b = lax.ppermute(add(down2_b, above_b[0]), "expert", down)
    total_b = jnp.stack([add(keep_b[0], above_b[1], up3_b), add(keep_b[1], below_b[1], down3_b)])
    (total_b,) = after((total_b,), back_a)
    back_b = leave(total_b, sizes[1])
    return combine(mixed, expert_gate, place, [back_a, back_b])


def solution(mesh):
    in_specs = (
        P(("tm", "expert"), None),
        P(None, ("tm", "expert"), None),
        P(),
        P(),
        P(),
        P(("tm", "expert")),
        P(("tm", "expert")),
        P(("tm", "expert")),
        P(("tm", "expert")),
        P(("tm", "expert")),
        P("tm", None, "expert"),
        P("tm", "expert", None),
    )
    out_specs = P(("tm", "expert"), None)
    return jax.shard_map(
        on_device, mesh=mesh, in_specs=in_specs, out_specs=out_specs, check_vma=False
    )
```

```python
import functools

import jax
import jax.numpy as jnp
from jax import lax
from jax.experimental import pallas as pl
from jax.experimental.pallas import tpu as pltpu
from jax.sharding import PartitionSpec as P

HEAD = 64
PAIR = 2 * HEAD
HALF = 256
TILE = 128
SPAN = 2 * HALF + TILE
EDGE = 16
GROUPS = (8, 4)
SIDE = 2
BLOCK = SIDE * PAIR
MIB = 1024 * 1024
STEP = 512
F32 = jnp.float32
BF16 = jnp.bfloat16


def call(body, out_shape, cost, vmem, **kw):
    flops, moved = cost
    return pl.pallas_call(
        body,
        out_shape=out_shape,
        cost_estimate=pl.CostEstimate(flops=flops, bytes_accessed=moved, transcendentals=0),
        compiler_params=pltpu.CompilerParams(vmem_limit_bytes=vmem * MIB),
        **kw,
    )


def fill_bias(edge_ref, bias):
    @pl.when(pl.program_id(0) == 0)
    def _():
        row = lax.broadcasted_iota(jnp.int32, (TILE, SPAN), 0)
        col = lax.broadcasted_iota(jnp.int32, (TILE, SPAN), 1)
        for r in range(2):
            low = jnp.where(edge_ref[0] == 1, HALF - TILE * r, 0)
            high = jnp.where(edge_ref[1] == 1, 2 * HALF - TILE * r, SPAN)
            kept = (col > row) & (col - row < 2 * HALF) & (col >= low) & (col < high)
            bias[r] = jnp.where(kept, 0.0, -1e30)


def attend_pairs(q_ref, kv_ref, lo_ref, hi_ref, bias, put):
    lane = lax.broadcasted_iota(jnp.int32, (1, PAIR), 1)
    first = lane < HEAD
    only0 = jnp.where(first, 0.125, 0.0).astype(BF16)
    only1 = jnp.where(first, 0.0, 0.125).astype(BF16)
    ones = jnp.ones((SPAN, PAIR), BF16)
    for c in range(SIDE):
        cols = slice(c * PAIR, (c + 1) * PAIR)
        for r in range(2):
            if r == 0:
                join = lambda i: [lo_ref[i, :, cols], kv_ref[i, :, cols], hi_ref[i, :TILE, cols]]
            else:
                join = lambda i: [lo_ref[i, TILE:, cols], kv_ref[i, :, cols], hi_ref[i, :, cols]]
            rows = slice(r * TILE, (r + 1) * TILE)
            q = q_ref[rows, cols]
            both = jnp.concatenate([q * only0, q * only1], axis=0)
            s = lax.dot_general(
                both,
                jnp.concatenate(join(0), axis=0),
                (((1,), (1,)), ((), ())),
                preferred_element_type=F32,
            )
            s = s + jnp.concatenate([bias[r], bias[r]], axis=0)
            p = jnp.exp(s - jnp.max(s, axis=1, keepdims=True)).astype(BF16)
            values = jnp.concatenate([jnp.concatenate(join(1), axis=0), ones], axis=1)
            o = jnp.dot(p, values, preferred_element_type=F32)
            o = o[:, :PAIR] / o[:, PAIR:]
            put(c, rows, jnp.where(first, o[:TILE], o[TILE:]))


def attend_body(edge_ref, q_ref, kv_ref, lo_ref, hi_ref, out_ref, bias):
    fill_bias(edge_ref, bias)

    def put(c, rows, value):
        out_ref[rows, c * PAIR : (c + 1) * PAIR] = value

    attend_pairs(q_ref, kv_ref, lo_ref, hi_ref, bias, put)


def attend_norm_body(groups, edge_ref, q_ref, kv_ref, lo_ref, hi_ref, gain_ref, *rest):
    n = len(groups)
    earlier, (out_ref, low_ref, high_ref, bias, mine) = rest[:n], rest[n:]
    step = pl.program_id(0)
    fill_bias(edge_ref, bias)

    def put(c, rows, value):
        mine[step * SIDE + c, rows] = value

    attend_pairs(q_ref, kv_ref, lo_ref, hi_ref, bias, put)

    @pl.when(step == pl.num_programs(0) - 1)
    def _():
        blocks = [(ref, c) for ref, g in zip(earlier, groups) for c in range(g)]
        pieces = [(lambda ref=ref, c=c: ref[:, c * PAIR : (c + 1) * PAIR]) for ref, c in blocks]
        pieces += [(lambda c=c: mine[c]) for c in range(mine.shape[0])]
        total = jnp.zeros((2 * TILE, PAIR), F32)
        for piece in pieces:
            v = piece()
            total = total + v * v
        width = len(pieces) * PAIR
        scale = lax.rsqrt(jnp.sum(total, axis=1, keepdims=True) * (1.0 / width) + 1e-6)
        for c, piece in enumerate(pieces):
            cols = slice(c * PAIR, (c + 1) * PAIR)
            out_ref[:, cols] = (piece() * scale * gain_ref[:, cols]).astype(BF16)
        low_ref[...] = out_ref[:EDGE]
        high_ref[...] = out_ref[2 * TILE - EDGE :]


def attention(queries, key_value, low, high, edge, conv_gain):
    rows, width = queries.shape
    outs = []
    start = 0
    for g, pairs in enumerate(GROUPS):
        last = g == len(GROUPS) - 1
        base = [
            pl.BlockSpec(memory_space=pltpu.SMEM),
            pl.BlockSpec((rows, BLOCK), lambda j, s=start // SIDE: (0, s + j)),
            pl.BlockSpec((2, rows, BLOCK), lambda j, s=start // SIDE: (0, 0, s + j)),
            pl.BlockSpec((2, rows, BLOCK), lambda j: (0, 0, j)),
            pl.BlockSpec((2, rows, BLOCK), lambda j: (0, 0, j)),
        ]
        scratch = [pltpu.VMEM((2, TILE, SPAN), F32)]
        cost = (pairs * 16 * rows * SPAN * PAIR, pairs * 7 * rows * PAIR * 2)
        before, after = low[g], high[g]
        if outs:
            before, after, _ = lax.optimization_barrier((before, after, outs[-1]))
        args = (edge, queries, key_value, before, after)
        if not last:
            outs.append(
                call(
                    attend_body,
                    jax.ShapeDtypeStruct((rows, pairs * PAIR), F32),
                    cost,
                    16,
                    grid=(pairs // SIDE,),
                    in_specs=base,
                    out_specs=pl.BlockSpec((rows, BLOCK), lambda j: (0, j)),
                    scratch_shapes=scratch,
                )(*args)
            )
        else:
            whole = lambda *shape: pl.BlockSpec(shape, lambda j: (0,) * len(shape))
            return call(
                functools.partial(attend_norm_body, GROUPS[:-1]),
                [
                    jax.ShapeDtypeStruct((rows, width), BF16),
                    jax.ShapeDtypeStruct((EDGE, width), BF16),
                    jax.ShapeDtypeStruct((EDGE, width), BF16),
                ],
                cost,
                20,
                grid=(pairs // SIDE,),
                in_specs=base + [whole(1, width)] + [whole(*o.shape) for o in outs],
                out_specs=[whole(rows, width), whole(EDGE, width), whole(EDGE, width)],
                scratch_shapes=scratch + [pltpu.VMEM((pairs, rows, PAIR), F32)],
            )(*args, conv_gain[None], *outs)
        start += pairs


def silu(v):
    half = 0.5 * v
    return half + half * jnp.tanh(half)


def conv_rows(source, taps, first, count):
    total = jnp.zeros((count, PAIR), F32)
    for k in range(taps.shape[0]):
        total = total + taps[k : k + 1] * source[first + k : first + k + count]
    return source[first + 15 : first + 15 + count] + silu(total)


def inner_conv_body(normed_ref, taps_ref, out_ref, wide):
    wide[...] = normed_ref[...].astype(F32)
    count = 32
    for t in range(0, out_ref.shape[0], count):
        out_ref[t : t + count] = conv_rows(wide, taps_ref, EDGE + t - 15, count).astype(BF16)


def inner_conv(normed, taps):
    rows, width = normed.shape
    inner = rows - 2 * EDGE
    return call(
        inner_conv_body,
        jax.ShapeDtypeStruct((inner, width), BF16),
        (62 * inner * width * 64, 4 * rows * width),
        16,
        grid=(width // PAIR,),
        in_specs=[
            pl.BlockSpec((rows, PAIR), lambda j: (0, j)),
            pl.BlockSpec((taps.shape[0], PAIR), lambda j: (0, j)),
        ],
        out_specs=pl.BlockSpec((inner, PAIR), lambda j: (0, j)),
        scratch_shapes=[pltpu.VMEM((rows, PAIR), F32)],
    )(normed, taps)


def dispatch_body(normed_ref, inner_ref, low_ref, high_ref, taps_ref, gain_ref, place_ref, *rest):
    mixed_ref, outs, (wide,) = rest[0], rest[1:-1], rest[-1:]
    rows, width = normed_ref.shape
    for c in range(width // PAIR):
        cols = slice(c * PAIR, (c + 1) * PAIR)
        wide[0, :EDGE] = low_ref[:, cols].astype(F32)
        wide[0, EDGE:] = normed_ref[: 2 * EDGE, cols].astype(F32)
        wide[1, : 2 * EDGE] = normed_ref[rows - 2 * EDGE :, cols].astype(F32)
        wide[1, 2 * EDGE :] = high_ref[:, cols].astype(F32)
        taps = taps_ref.at[:, cols]
        mixed_ref[:EDGE, cols] = conv_rows(wide.at[0], taps, 1, EDGE).astype(BF16)
        mixed_ref[rows - EDGE :, cols] = conv_rows(wide.at[1], taps, 1, EDGE).astype(BF16)
    mixed_ref[EDGE : rows - EDGE] = inner_ref[...]
    mixed = mixed_ref[...].astype(F32)
    scale = lax.rsqrt(jnp.mean(mixed * mixed, axis=1, keepdims=True) + 1e-6)
    expert_in = (mixed * scale * gain_ref[...]).astype(BF16)
    first = 0
    for out_ref in outs:
        count = out_ref.shape[0]
        place = first + lax.broadcasted_iota(jnp.int32, (count, rows), 0)
        pick = jnp.where(place == place_ref[...], 1.0, 0.0).astype(BF16)
        out_ref[...] = jnp.dot(pick, expert_in, preferred_element_type=F32).astype(BF16)
        first += count


def dispatch(normed, inner, low, high, taps, gain, place, counts):
    rows, width = normed.shape
    return call(
        dispatch_body,
        [jax.ShapeDtypeStruct((rows, width), BF16)]
        + [jax.ShapeDtypeStruct((count, width), BF16) for count in counts],
        (2 * sum(counts) * rows * width, 8 * rows * width),
        24,
        scratch_shapes=[pltpu.VMEM((2, 3 * EDGE, PAIR), F32)],
    )(normed, inner, low, high, taps, gain[None], place[None])


def combine_body(mixed_ref, gate_ref, place_ref, *rest):
    parts, out_ref = rest[:-1], rest[-1]
    rows = mixed_ref.shape[0]
    total = None
    first = 0
    for part in parts:
        count = part.shape[0]
        place = first + lax.broadcasted_iota(jnp.int32, (rows, count), 1)
        pick = jnp.where(place == place_ref[...], 1.0, 0.0).astype(BF16)
        got = jnp.dot(pick, part[...], preferred_element_type=F32)
        total = got if total is None else total + got
        first += count
    out_ref[...] = (mixed_ref[...].astype(F32) + gate_ref[...] * total).astype(BF16)


def combine(mixed, gate, place, parts):
    rows, width = mixed.shape
    block = 256
    column = lambda n: pl.BlockSpec((n, block), lambda j: (0, j))
    fixed = pl.BlockSpec((rows, 1), lambda j: (0, 0))
    return call(
        combine_body,
        jax.ShapeDtypeStruct((rows, width), BF16),
        (2 * sum(p.shape[0] for p in parts) * rows * width, 8 * rows * width),
        16,
        grid=(width // block,),
        in_specs=[column(rows), fixed, fixed] + [column(p.shape[0]) for p in parts],
        out_specs=column(rows),
    )(mixed, gate[:, None], place[:, None], *parts)


def ffn_body(direct, own, left, right, *rest):
    if direct:
        far, w_in, w_out, keep, to_right, to_left, to_far, *scratch = rest
        far0, far1 = far.at[0], far.at[1]
    else:
        far0, far1, w_in, w_out, keep, up, down, up2, down2, *scratch = rest
    rows_in, hidden, first, second, sems = scratch
    n, width = own.shape[1:]
    units = hidden.shape[1]
    step = STEP
    copies = {}
    for e in range(2):
        for which, (weight, held) in enumerate(((w_in, first), (w_out, second))):
            for t in range(weight.shape[2] // step):
                cols = slice(t * step, (t + 1) * step)
                copies[e, which, t] = pltpu.make_async_copy(
                    weight.at[e, :, cols], held.at[e, t], sems.at[e, which, t]
                )
                copies[e, which, t].start()
    for e in range(2):
        rows_in[:n] = own[e]
        rows_in[n : 2 * n] = left[e]
        rows_in[2 * n : 3 * n] = right[e]
        rows_in[3 * n :] = (far0 if e == 0 else far1)[...]
        for t in range(units // step):
            copies[e, 0, t].wait()
            part = jnp.dot(rows_in[...], first[e, t], preferred_element_type=F32)
            hidden[:, t * step : (t + 1) * step] = silu(part).astype(BF16)
        for t in range(width // step):
            copies[e, 1, t].wait()
            cols = slice(t * step, (t + 1) * step)
            part = jnp.dot(hidden[...], second[e, t], preferred_element_type=F32).astype(BF16)
            keep[e, :, cols] = part[:n]
            if direct:
                to_left[e, :, cols] = part[n : 2 * n]
                to_right[e, :, cols] = part[2 * n : 3 * n]
                to_far[e, :, cols] = part[3 * n :]
            elif e == 0:
                down[1, :, cols] = part[n : 2 * n]
                up2[:, cols] = part[2 * n : 3 * n]
                up[0, :, cols] = part[3 * n :]
            else:
                down2[:, cols] = part[n : 2 * n]
                up[1, :, cols] = part[2 * n : 3 * n]
                down[0, :, cols] = part[3 * n :]


def ffn(own, left, right, far, w_in, w_out):
    direct = len(far) == 1
    experts, n, width = own.shape
    units = w_in.shape[2]
    pair = jax.ShapeDtypeStruct((2, n, width), BF16)
    single = jax.ShapeDtypeStruct((n, width), BF16)
    return call(
        functools.partial(ffn_body, direct),
        [pair] * 4 if direct else [pair, pair, pair, single, single],
        (experts * 4 * n * width * units * 4, 2 * experts * width * units * 2),
        50,
        in_specs=[pl.BlockSpec(memory_space=pltpu.VMEM)] * (3 + len(far)) + [pl.BlockSpec(memory_space=pl.ANY)] * 2,
        scratch_shapes=[
            pltpu.VMEM((4 * n, width), BF16),
            pltpu.VMEM((4 * n, units), BF16),
            pltpu.VMEM((2, units // STEP, width, STEP), BF16),
            pltpu.VMEM((2, width // STEP, units, STEP), BF16),
            pltpu.SemaphoreType.DMA((2, 2, max(units, width) // STEP)),
        ],
    )(own, left, right, *far, w_in, w_out)


def on_device(
    queries,
    key_value,
    conv_kernel,
    conv_gain,
    ffn_gain,
    expert_gate,
    primary,
    secondary,
    overflow,
    slot,
    w_in,
    w_out,
):
    frame_rows, width = queries.shape
    time_count = lax.axis_size("tm")
    group_count = lax.axis_size("expert")
    devices = time_count * group_count
    index = lax.axis_index("tm") * group_count + lax.axis_index("expert")
    edge = jnp.stack([index == 0, index == devices - 1]).astype(jnp.int32)
    order = ("tm", "expert")
    onward = [(i, i + 1) for i in range(devices - 1)]
    back = [(i + 1, i) for i in range(devices - 1)]

    low, high = [], []
    start = 0
    source = key_value
    for pairs in GROUPS:
        part = lax.slice_in_dim(source, start * PAIR, (start + pairs) * PAIR, axis=2)
        low.append(lax.ppermute(part, order, onward))
        high.append(lax.ppermute(part, order, back))
        start += pairs
        source, _ = lax.optimization_barrier((key_value, part))
    normed, first_rows, last_rows = attention(queries, key_value, low, high, edge, conv_gain)

    before = lax.ppermute(last_rows, order, onward)
    after = lax.ppermute(first_rows, order, back)
    inner = inner_conv(normed, conv_kernel)

    local = w_in.shape[0]
    experts = local * time_count
    slots = max(2, 3 * frame_rows // (2 * experts))
    early = 2 * slots // 3
    sizes = (early, slots - early)
    served = jnp.where(overflow == 1, secondary, primary)
    place = jnp.where(
        slot < early,
        served * early + slot,
        experts * early + served * (slots - early) + slot - early,
    )
    mixed, *chunks = dispatch(
        normed, inner, before, after, conv_kernel, ffn_gain, place, [experts * c for c in sizes]
    )

    up = [(i, (i + 1) % group_count) for i in range(group_count)]
    down = [((i + 1) % group_count, i) for i in range(group_count)]
    add = lambda *vs: sum(v.astype(F32) for v in vs).astype(BF16)

    def arrive(chunk, size):
        sent = chunk.reshape(time_count, local * size, width)
        own = lax.all_to_all(sent, "tm", split_axis=0, concat_axis=0, tiled=True)
        own = own.reshape(time_count, local, size, width).transpose(1, 0, 2, 3)
        return own.reshape(local, time_count * size, width)

    def near(own):
        return lax.ppermute(own, "expert", up), lax.ppermute(own, "expert", down)

    def far(halves):
        return lax.ppermute(halves[0], "expert", up), lax.ppermute(halves[1], "expert", down)

    def home(summed, size):
        summed = summed.reshape(local, time_count, size, width).transpose(1, 0, 2, 3)
        return summed.reshape(time_count, local * size, width)

    def leave(summed, size):
        got = lax.all_to_all(summed, "tm", split_axis=0, concat_axis=0, tiled=True)
        return got.reshape(experts * size, width)

    after = lambda values, *others: lax.optimization_barrier((tuple(values), others))[0]
    own_a = arrive(chunks[0], sizes[0])
    left_a, right_a = near(own_a)
    own_b = arrive(*after((chunks[1],), own_a), sizes[1])
    left_a, right_a = after((left_a, right_a), own_b)
    far_a = far((left_a[0], right_a[1]))
    left_b, right_b = near(own_b)
    across = [(i, (i + 2) % group_count) for i in range(group_count)]
    far_b = lax.ppermute(own_b, "expert", across)
    keep_a, go_up_a, go_down_a, up2_a, down2_a = ffn(own_a, left_a, right_a, far_a, w_in, w_out)
    below_a, above_a = lax.ppermute(go_up_a, "expert", up), lax.ppermute(go_down_a, "expert", down)
    (own_b,) = after((own_b,), keep_a)
    keep_b, to_right, to_left, to_far = ffn(own_b, left_b, right_b, (far_b,), w_in, w_out)
    below_a, above_a = after((below_a, above_a), keep_b)
    up2_a, down2_a = add(up2_a, below_a[0]), add(down2_a, above_a[0])
    up3_a, down3_a = lax.ppermute(up2_a, "expert", up), lax.ppermute(down2_a, "expert", down)
    to_right, to_left, to_far = after((to_right, to_left, to_far), up3_a, down3_a)
    parts_b = (
        lax.ppermute(to_right, "expert", up),
        lax.ppermute(to_left, "expert", down),
        lax.ppermute(to_far, "expert", across),
    )
    total_a = jnp.stack([add(keep_a[0], above_a[1], up3_a), add(keep_a[1], below_a[1], down3_a)])
    back_a = leave(home(total_a, sizes[0]), sizes[0])
    parts_b = after(parts_b, back_a)
    back_b = leave(home(add(keep_b, *parts_b), sizes[1]), sizes[1])
    return combine(mixed, expert_gate, place, [back_a, back_b])


def solution(mesh):
    in_specs = (
        P(("tm", "expert"), None),
        P(None, ("tm", "expert"), None),
        P(),
        P(),
        P(),
        P(("tm", "expert")),
        P(("tm", "expert")),
        P(("tm", "expert")),
        P(("tm", "expert")),
        P(("tm", "expert")),
        P("tm", None, "expert"),
        P("tm", "expert", None),
    )
    out_specs = P(("tm", "expert"), None)
    return jax.shard_map(
        on_device, mesh=mesh, in_specs=in_specs, out_specs=out_specs, check_vma=False
    )
```

```python
import functools

import jax
import jax.numpy as jnp
from jax import lax
from jax.experimental import pallas as pl
from jax.experimental.pallas import tpu as pltpu
from jax.sharding import PartitionSpec as P

HEAD = 64
PAIR = 2 * HEAD
HALF = 256
TILE = 128
SPAN = 2 * HALF + TILE
EDGE = 16
GROUPS = (6, 6)
SIDE = 2
BLOCK = SIDE * PAIR
MIB = 1024 * 1024
STEP = 512
F32 = jnp.float32
BF16 = jnp.bfloat16


def call(body, out_shape, cost, vmem, **kw):
    flops, moved = cost
    return pl.pallas_call(
        body,
        out_shape=out_shape,
        cost_estimate=pl.CostEstimate(flops=flops, bytes_accessed=moved, transcendentals=0),
        compiler_params=pltpu.CompilerParams(vmem_limit_bytes=vmem * MIB),
        **kw,
    )


def fill_bias(edge_ref, bias):
    @pl.when(pl.program_id(0) == 0)
    def _():
        row = lax.broadcasted_iota(jnp.int32, (TILE, SPAN), 0)
        col = lax.broadcasted_iota(jnp.int32, (TILE, SPAN), 1)
        for r in range(2):
            low = jnp.where(edge_ref[0] == 1, HALF - TILE * r, 0)
            high = jnp.where(edge_ref[1] == 1, 2 * HALF - TILE * r, SPAN)
            kept = (col > row) & (col - row < 2 * HALF) & (col >= low) & (col < high)
            bias[r] = jnp.where(kept, 0.0, -1e30)


def attend_pairs(q_ref, kv_ref, lo_ref, hi_ref, bias, put):
    lane = lax.broadcasted_iota(jnp.int32, (1, PAIR), 1)
    first = lane < HEAD
    only0 = jnp.where(first, 0.125, 0.0).astype(BF16)
    only1 = jnp.where(first, 0.0, 0.125).astype(BF16)
    ones = jnp.ones((SPAN, PAIR), BF16)
    for c in range(SIDE):
        cols = slice(c * PAIR, (c + 1) * PAIR)
        for r in range(2):
            if r == 0:
                join = lambda i: [lo_ref[i, :, cols], kv_ref[i, :, cols], hi_ref[i, :TILE, cols]]
            else:
                join = lambda i: [lo_ref[i, TILE:, cols], kv_ref[i, :, cols], hi_ref[i, :, cols]]
            rows = slice(r * TILE, (r + 1) * TILE)
            q = q_ref[rows, cols]
            both = jnp.concatenate([q * only0, q * only1], axis=0)
            s = lax.dot_general(
                both,
                jnp.concatenate(join(0), axis=0),
                (((1,), (1,)), ((), ())),
                preferred_element_type=F32,
            )
            s = s + jnp.concatenate([bias[r], bias[r]], axis=0)
            p = jnp.exp(s - jnp.max(s, axis=1, keepdims=True)).astype(BF16)
            values = jnp.concatenate([jnp.concatenate(join(1), axis=0), ones], axis=1)
            o = jnp.dot(p, values, preferred_element_type=F32)
            o = o[:, :PAIR] / o[:, PAIR:]
            put(c, rows, jnp.where(first, o[:TILE], o[TILE:]))


def attend_body(edge_ref, q_ref, kv_ref, lo_ref, hi_ref, out_ref, bias):
    fill_bias(edge_ref, bias)

    def put(c, rows, value):
        out_ref[rows, c * PAIR : (c + 1) * PAIR] = value

    attend_pairs(q_ref, kv_ref, lo_ref, hi_ref, bias, put)


def attend_norm_body(groups, edge_ref, q_ref, kv_ref, lo_ref, hi_ref, gain_ref, *rest):
    n = len(groups)
    earlier, (out_ref, low_ref, high_ref, bias, mine) = rest[:n], rest[n:]
    step = pl.program_id(0)
    fill_bias(edge_ref, bias)

    def put(c, rows, value):
        mine[step * SIDE + c, rows] = value

    attend_pairs(q_ref, kv_ref, lo_ref, hi_ref, bias, put)

    @pl.when(step == pl.num_programs(0) - 1)
    def _():
        blocks = [(ref, c) for ref, g in zip(earlier, groups) for c in range(g)]
        pieces = [(lambda ref=ref, c=c: ref[:, c * PAIR : (c + 1) * PAIR]) for ref, c in blocks]
        pieces += [(lambda c=c: mine[c]) for c in range(mine.shape[0])]
        total = jnp.zeros((2 * TILE, PAIR), F32)
        for piece in pieces:
            v = piece()
            total = total + v * v
        width = len(pieces) * PAIR
        scale = lax.rsqrt(jnp.sum(total, axis=1, keepdims=True) * (1.0 / width) + 1e-6)
        for c, piece in enumerate(pieces):
            cols = slice(c * PAIR, (c + 1) * PAIR)
            out_ref[:, cols] = (piece() * scale * gain_ref[:, cols]).astype(BF16)
        low_ref[...] = out_ref[:EDGE]
        high_ref[...] = out_ref[2 * TILE - EDGE :]


def attention(queries, key_value, low, high, edge, conv_gain):
    rows, width = queries.shape
    outs = []
    start = 0
    for g, pairs in enumerate(GROUPS):
        last = g == len(GROUPS) - 1
        base = [
            pl.BlockSpec(memory_space=pltpu.SMEM),
            pl.BlockSpec((rows, BLOCK), lambda j, s=start // SIDE: (0, s + j)),
            pl.BlockSpec((2, rows, BLOCK), lambda j, s=start // SIDE: (0, 0, s + j)),
            pl.BlockSpec((2, rows, BLOCK), lambda j: (0, 0, j)),
            pl.BlockSpec((2, rows, BLOCK), lambda j: (0, 0, j)),
        ]
        scratch = [pltpu.VMEM((2, TILE, SPAN), F32)]
        cost = (pairs * 16 * rows * SPAN * PAIR, pairs * 7 * rows * PAIR * 2)
        before, after = low[g], high[g]
        if outs:
            before, after, _ = lax.optimization_barrier((before, after, outs[-1]))
        args = (edge, queries, key_value, before, after)
        if not last:
            outs.append(
                call(
                    attend_body,
                    jax.ShapeDtypeStruct((rows, pairs * PAIR), F32),
                    cost,
                    58,
                    grid=(pairs // SIDE,),
                    in_specs=base,
                    out_specs=pl.BlockSpec((rows, BLOCK), lambda j: (0, j)),
                    scratch_shapes=scratch,
                )(*args)
            )
        else:
            whole = lambda *shape: pl.BlockSpec(shape, lambda j: (0,) * len(shape))
            return call(
                functools.partial(attend_norm_body, GROUPS[:-1]),
                [
                    jax.ShapeDtypeStruct((rows, width), BF16),
                    jax.ShapeDtypeStruct((EDGE, width), BF16),
                    jax.ShapeDtypeStruct((EDGE, width), BF16),
                ],
                cost,
                58,
                grid=(pairs // SIDE,),
                in_specs=base + [whole(1, width)] + [whole(*o.shape) for o in outs],
                out_specs=[whole(rows, width), whole(EDGE, width), whole(EDGE, width)],
                scratch_shapes=scratch + [pltpu.VMEM((pairs, rows, PAIR), F32)],
            )(*args, conv_gain[None], *outs)
        start += pairs


def silu(v):
    half = 0.5 * v
    return half + half * jnp.tanh(half)


def conv_rows(source, taps, first, count):
    total = jnp.zeros((count, PAIR), F32)
    for k in range(taps.shape[0]):
        total = total + taps[k : k + 1] * source[first + k : first + k + count]
    return source[first + 15 : first + 15 + count] + silu(total)


def inner_conv_body(normed_ref, taps_ref, out_ref, wide):
    wide[...] = normed_ref[...].astype(F32)
    count = 32
    for t in range(0, out_ref.shape[0], count):
        out_ref[t : t + count] = conv_rows(wide, taps_ref, EDGE + t - 15, count).astype(BF16)


def inner_conv(normed, taps):
    rows, width = normed.shape
    inner = rows - 2 * EDGE
    return call(
        inner_conv_body,
        jax.ShapeDtypeStruct((inner, width), BF16),
        (62 * inner * width * 64, 4 * rows * width),
        16,
        grid=(width // PAIR,),
        in_specs=[
            pl.BlockSpec((rows, PAIR), lambda j: (0, j)),
            pl.BlockSpec((taps.shape[0], PAIR), lambda j: (0, j)),
        ],
        out_specs=pl.BlockSpec((inner, PAIR), lambda j: (0, j)),
        scratch_shapes=[pltpu.VMEM((rows, PAIR), F32)],
    )(normed, taps)


def dispatch_body(normed_ref, inner_ref, low_ref, high_ref, taps_ref, gain_ref, place_ref, *rest):
    mixed_ref, outs, (wide,) = rest[0], rest[1:-1], rest[-1:]
    rows, width = normed_ref.shape
    for c in range(width // PAIR):
        cols = slice(c * PAIR, (c + 1) * PAIR)
        wide[0, :EDGE] = low_ref[:, cols].astype(F32)
        wide[0, EDGE:] = normed_ref[: 2 * EDGE, cols].astype(F32)
        wide[1, : 2 * EDGE] = normed_ref[rows - 2 * EDGE :, cols].astype(F32)
        wide[1, 2 * EDGE :] = high_ref[:, cols].astype(F32)
        taps = taps_ref.at[:, cols]
        mixed_ref[:EDGE, cols] = conv_rows(wide.at[0], taps, 1, EDGE).astype(BF16)
        mixed_ref[rows - EDGE :, cols] = conv_rows(wide.at[1], taps, 1, EDGE).astype(BF16)
    mixed_ref[EDGE : rows - EDGE] = inner_ref[...]
    mixed = mixed_ref[...].astype(F32)
    scale = lax.rsqrt(jnp.mean(mixed * mixed, axis=1, keepdims=True) + 1e-6)
    expert_in = (mixed * scale * gain_ref[...]).astype(BF16)
    first = 0
    for out_ref in outs:
        count = out_ref.shape[0]
        place = first + lax.broadcasted_iota(jnp.int32, (count, rows), 0)
        pick = jnp.where(place == place_ref[...], 1.0, 0.0).astype(BF16)
        out_ref[...] = jnp.dot(pick, expert_in, preferred_element_type=F32).astype(BF16)
        first += count


def dispatch(normed, inner, low, high, taps, gain, place, counts):
    rows, width = normed.shape
    return call(
        dispatch_body,
        [jax.ShapeDtypeStruct((rows, width), BF16)]
        + [jax.ShapeDtypeStruct((count, width), BF16) for count in counts],
        (2 * sum(counts) * rows * width, 8 * rows * width),
        24,
        scratch_shapes=[pltpu.VMEM((2, 3 * EDGE, PAIR), F32)],
    )(normed, inner, low, high, taps, gain[None], place[None])


def combine_body(counts, mixed_ref, gate_ref, place_ref, *rest):
    parts, out_ref = rest[:-1], rest[-1]
    rows = mixed_ref.shape[0]
    total = None
    first = 0
    for part, count in zip(parts, counts):
        times = part.shape[0] // count
        place = first + lax.broadcasted_iota(jnp.int32, (rows, count), 1)
        pick = jnp.where(place == place_ref[...], 1.0, 0.0).astype(BF16)
        got = jnp.dot(
            jnp.concatenate([pick] * times, axis=1), part[...], preferred_element_type=F32
        )
        total = got if total is None else total + got
        first += count
    picked = total.astype(BF16).astype(F32)
    out_ref[...] = (mixed_ref[...].astype(F32) + gate_ref[...] * picked).astype(BF16)


def combine(mixed, gate, place, parts, counts):
    rows, width = mixed.shape
    block = 256
    column = lambda n: pl.BlockSpec((n, block), lambda j: (0, j))
    fixed = pl.BlockSpec((rows, 1), lambda j: (0, 0))
    return call(
        functools.partial(combine_body, counts),
        jax.ShapeDtypeStruct((rows, width), BF16),
        (2 * sum(p.shape[0] for p in parts) * rows * width, 8 * rows * width),
        16,
        grid=(width // block,),
        in_specs=[column(rows), fixed, fixed] + [column(p.shape[0]) for p in parts],
        out_specs=column(rows),
    )(mixed, gate[:, None], place[:, None], *parts)


def ffn_body(direct, own, left, right, *rest):
    if direct:
        far, me, w_in, w_out, out, *scratch = rest
        places = [(me[0] + k) % 4 for k in (0, 3, 1, 2)]
        far0, far1 = far.at[0], far.at[1]
    else:
        far0, far1, w_in, w_out, keep, up, down, up2, down2, *scratch = rest
    rows_in, hidden, first, second, sems = scratch
    n, width = own.shape[1:]
    units = hidden.shape[1]
    step = STEP
    copies = {}
    for e in range(2):
        for which, (weight, held) in enumerate(((w_in, first), (w_out, second))):
            for t in range(weight.shape[2] // step):
                cols = slice(t * step, (t + 1) * step)
                copies[e, which, t] = pltpu.make_async_copy(
                    weight.at[e, :, cols], held.at[e, t], sems.at[e, which, t]
                )
                copies[e, which, t].start()
    for e in range(2):
        rows_in[:n] = own[e]
        rows_in[n : 2 * n] = left[e]
        rows_in[2 * n : 3 * n] = right[e]
        rows_in[3 * n :] = (far0 if e == 0 else far1)[...]
        for t in range(units // step):
            copies[e, 0, t].wait()
            part = jnp.dot(rows_in[...], first[e, t], preferred_element_type=F32)
            hidden[:, t * step : (t + 1) * step] = silu(part).astype(BF16)
        for t in range(width // step):
            copies[e, 1, t].wait()
            cols = slice(t * step, (t + 1) * step)
            part = jnp.dot(hidden[...], second[e, t], preferred_element_type=F32).astype(BF16)
            if direct:
                for k, at in enumerate(places):
                    out[at, e, :, cols] = part[k * n : (k + 1) * n]
                continue
            keep[e, :, cols] = part[:n]
            if e == 0:
                down[1, :, cols] = part[n : 2 * n]
                up2[:, cols] = part[2 * n : 3 * n]
                up[0, :, cols] = part[3 * n :]
            else:
                down2[:, cols] = part[n : 2 * n]
                up[1, :, cols] = part[2 * n : 3 * n]
                down[0, :, cols] = part[3 * n :]


def ffn(own, left, right, far, w_in, w_out, me=None):
    direct = me is not None
    experts, n, width = own.shape
    units = w_in.shape[2]
    pair = jax.ShapeDtypeStruct((2, n, width), BF16)
    single = jax.ShapeDtypeStruct((n, width), BF16)
    return call(
        functools.partial(ffn_body, direct),
        jax.ShapeDtypeStruct((4, 2, n, width), BF16) if direct else [pair, pair, pair, single, single],
        (experts * 4 * n * width * units * 4, 2 * experts * width * units * 2),
        50,
        in_specs=[pl.BlockSpec(memory_space=pltpu.VMEM)] * (3 + len(far))
        + [pl.BlockSpec(memory_space=pltpu.SMEM)] * direct
        + [pl.BlockSpec(memory_space=pl.ANY)] * 2,
        scratch_shapes=[
            pltpu.VMEM((4 * n, width), BF16),
            pltpu.VMEM((4 * n, units), BF16),
            pltpu.VMEM((2, units // STEP, width, STEP), BF16),
            pltpu.VMEM((2, width // STEP, units, STEP), BF16),
            pltpu.SemaphoreType.DMA((2, 2, max(units, width) // STEP)),
        ],
    )(own, left, right, *far, *([me] if direct else []), w_in, w_out)


def on_device(
    queries,
    key_value,
    conv_kernel,
    conv_gain,
    ffn_gain,
    expert_gate,
    primary,
    secondary,
    overflow,
    slot,
    w_in,
    w_out,
):
    frame_rows, width = queries.shape
    time_count = lax.axis_size("tm")
    group_count = lax.axis_size("expert")
    devices = time_count * group_count
    index = lax.axis_index("tm") * group_count + lax.axis_index("expert")
    edge = jnp.stack([index == 0, index == devices - 1]).astype(jnp.int32)
    order = ("tm", "expert")
    onward = [(i, i + 1) for i in range(devices - 1)]
    back = [(i + 1, i) for i in range(devices - 1)]

    low, high = [], []
    start = 0
    source = key_value
    for pairs in GROUPS:
        part = lax.slice_in_dim(source, start * PAIR, (start + pairs) * PAIR, axis=2)
        low.append(lax.ppermute(part, order, onward))
        high.append(lax.ppermute(part, order, back))
        start += pairs
        source, _ = lax.optimization_barrier((key_value, part))
    normed, first_rows, last_rows = attention(queries, key_value, low, high, edge, conv_gain)

    before = lax.ppermute(last_rows, order, onward)
    after = lax.ppermute(first_rows, order, back)
    inner = inner_conv(normed, conv_kernel)

    local = w_in.shape[0]
    experts = local * time_count
    slots = max(2, 3 * frame_rows // (2 * experts))
    early = 2 * slots // 3
    sizes = (early, slots - early)
    served = jnp.where(overflow == 1, secondary, primary)
    place = jnp.where(
        slot < early,
        served * early + slot,
        experts * early + served * (slots - early) + slot - early,
    )
    mixed, *chunks = dispatch(
        normed, inner, before, after, conv_kernel, ffn_gain, place, [experts * c for c in sizes]
    )

    up = [(i, (i + 1) % group_count) for i in range(group_count)]
    down = [((i + 1) % group_count, i) for i in range(group_count)]
    add = lambda *vs: sum(v.astype(F32) for v in vs).astype(BF16)

    def arrive(chunk, size):
        sent = chunk.reshape(time_count, local * size, width)
        own = lax.all_to_all(sent, "tm", split_axis=0, concat_axis=0, tiled=True)
        own = own.reshape(time_count, local, size, width).transpose(1, 0, 2, 3)
        return own.reshape(local, time_count * size, width)

    def near(own):
        return lax.ppermute(own, "expert", up), lax.ppermute(own, "expert", down)

    def far(halves):
        return lax.ppermute(halves[0], "expert", up), lax.ppermute(halves[1], "expert", down)

    def home(summed, size):
        summed = summed.reshape(local, time_count, size, width).transpose(1, 0, 2, 3)
        return summed.reshape(time_count, local * size, width)

    def leave(summed, size):
        got = lax.all_to_all(summed, "tm", split_axis=0, concat_axis=0, tiled=True)
        return got.reshape(experts * size, width)

    after = lambda values, *others: lax.optimization_barrier((tuple(values), others))[0]
    own_a = arrive(chunks[0], sizes[0])
    left_a, right_a = near(own_a)
    own_b = arrive(*after((chunks[1],), own_a), sizes[1])
    left_a, right_a = after((left_a, right_a), own_b)
    far_a = far((left_a[0], right_a[1]))
    left_b, right_b = near(own_b)
    across = [(i, (i + 2) % group_count) for i in range(group_count)]
    far_b = lax.ppermute(own_b, "expert", across)
    keep_a, go_up_a, go_down_a, up2_a, down2_a = ffn(own_a, left_a, right_a, far_a, w_in, w_out)
    below_a, above_a = lax.ppermute(go_up_a, "expert", up), lax.ppermute(go_down_a, "expert", down)
    (own_b,) = after((own_b,), keep_a)
    me = lax.axis_index("expert").astype(jnp.int32)[None]
    parts_b = ffn(own_b, left_b, right_b, (far_b,), w_in, w_out, me)
    parts_b = parts_b.reshape(group_count, local, time_count, sizes[1], width).transpose(0, 2, 1, 3, 4)
    parts_b = parts_b.reshape(devices, local * sizes[1], width)
    back_b = lax.all_to_all(parts_b, ("expert", "tm"), split_axis=0, concat_axis=0, tiled=True)
    back_b = back_b.reshape(group_count * experts * sizes[1], width)
    below_a, above_a = after((below_a, above_a), parts_b)
    up2_a, down2_a = add(up2_a, below_a[0]), add(down2_a, above_a[0])
    up3_a, down3_a = lax.ppermute(up2_a, "expert", up), lax.ppermute(down2_a, "expert", down)
    total_a = jnp.stack([add(keep_a[0], above_a[1], up3_a), add(keep_a[1], below_a[1], down3_a)])
    (total_a,) = after((home(total_a, sizes[0]),), back_b)
    back_a = leave(total_a, sizes[0])
    return combine(mixed, expert_gate, place, [back_a, back_b], [experts * c for c in sizes])


def solution(mesh):
    in_specs = (
        P(("tm", "expert"), None),
        P(None, ("tm", "expert"), None),
        P(),
        P(),
        P(),
        P(("tm", "expert")),
        P(("tm", "expert")),
        P(("tm", "expert")),
        P(("tm", "expert")),
        P(("tm", "expert")),
        P("tm", None, "expert"),
        P("tm", "expert", None),
    )
    out_specs = P(("tm", "expert"), None)
    return jax.shard_map(
        on_device, mesh=mesh, in_specs=in_specs, out_specs=out_specs, check_vma=False
    )
```

```python
import functools

import jax
import jax.numpy as jnp
from jax import lax
from jax.experimental import pallas as pl
from jax.experimental.pallas import tpu as pltpu
from jax.sharding import PartitionSpec as P

HEAD = 64
PAIR = 2 * HEAD
HALF = 256
TILE = 128
SPAN = 2 * HALF + TILE
EDGE = 16
GROUPS = (8, 4)
SIDE = 2
BLOCK = SIDE * PAIR
MIB = 1024 * 1024
STEP = 512
DEVICES = 32
F32 = jnp.float32
BF16 = jnp.bfloat16


def call(body, out_shape, cost, vmem, **kw):
    flops, moved = cost
    return pl.pallas_call(
        body,
        out_shape=out_shape,
        cost_estimate=pl.CostEstimate(flops=flops, bytes_accessed=moved, transcendentals=0),
        compiler_params=pltpu.CompilerParams(vmem_limit_bytes=vmem * MIB),
        **kw,
    )


def fill_bias(edge_ref, bias):
    @pl.when(pl.program_id(0) == 0)
    def _():
        row = lax.broadcasted_iota(jnp.int32, (TILE, SPAN), 0)
        col = lax.broadcasted_iota(jnp.int32, (TILE, SPAN), 1)
        for r in range(2):
            low = jnp.where(edge_ref[0] == 1, HALF - TILE * r, 0)
            high = jnp.where(edge_ref[1] == 1, 2 * HALF - TILE * r, SPAN)
            kept = (col > row) & (col - row < 2 * HALF) & (col >= low) & (col < high)
            bias[r] = jnp.where(kept, 0.0, -1e30)


def attend_pairs(q_ref, kv_ref, lo_ref, hi_ref, bias, put):
    lane = lax.broadcasted_iota(jnp.int32, (1, PAIR), 1)
    first = lane < HEAD
    only0 = jnp.where(first, 0.125, 0.0).astype(BF16)
    only1 = jnp.where(first, 0.0, 0.125).astype(BF16)
    ones = jnp.ones((SPAN, PAIR), BF16)
    for c in range(SIDE):
        cols = slice(c * PAIR, (c + 1) * PAIR)
        for r in range(2):
            if r == 0:
                join = lambda i: [lo_ref[i, :, cols], kv_ref[i, :, cols], hi_ref[i, :TILE, cols]]
            else:
                join = lambda i: [lo_ref[i, TILE:, cols], kv_ref[i, :, cols], hi_ref[i, :, cols]]
            rows = slice(r * TILE, (r + 1) * TILE)
            q = q_ref[rows, cols]
            both = jnp.concatenate([q * only0, q * only1], axis=0)
            s = lax.dot_general(
                both,
                jnp.concatenate(join(0), axis=0),
                (((1,), (1,)), ((), ())),
                preferred_element_type=F32,
            )
            s = s + jnp.concatenate([bias[r], bias[r]], axis=0)
            p = jnp.exp(s - jnp.max(s, axis=1, keepdims=True)).astype(BF16)
            values = jnp.concatenate([jnp.concatenate(join(1), axis=0), ones], axis=1)
            o = jnp.dot(p, values, preferred_element_type=F32)
            o = o[:, :PAIR] / o[:, PAIR:]
            put(c, rows, jnp.where(first, o[:TILE], o[TILE:]))


def attend_body(edge_ref, q_ref, kv_ref, lo_ref, hi_ref, out_ref, bias):
    fill_bias(edge_ref, bias)

    def put(c, rows, value):
        out_ref[rows, c * PAIR : (c + 1) * PAIR] = value

    attend_pairs(q_ref, kv_ref, lo_ref, hi_ref, bias, put)


def attend_norm_body(groups, edge_ref, q_ref, kv_ref, lo_ref, hi_ref, gain_ref, *rest):
    n = len(groups)
    earlier, (out_ref, low_ref, high_ref, bias, mine) = rest[:n], rest[n:]
    step = pl.program_id(0)
    fill_bias(edge_ref, bias)

    def put(c, rows, value):
        mine[step * SIDE + c, rows] = value

    attend_pairs(q_ref, kv_ref, lo_ref, hi_ref, bias, put)

    @pl.when(step == pl.num_programs(0) - 1)
    def _():
        blocks = [(ref, c) for ref, g in zip(earlier, groups) for c in range(g)]
        pieces = [(lambda ref=ref, c=c: ref[:, c * PAIR : (c + 1) * PAIR]) for ref, c in blocks]
        pieces += [(lambda c=c: mine[c]) for c in range(mine.shape[0])]
        total = jnp.zeros((2 * TILE, PAIR), F32)
        for piece in pieces:
            v = piece()
            total = total + v * v
        width = len(pieces) * PAIR
        scale = lax.rsqrt(jnp.sum(total, axis=1, keepdims=True) * (1.0 / width) + 1e-6)
        for c, piece in enumerate(pieces):
            cols = slice(c * PAIR, (c + 1) * PAIR)
            out_ref[:, cols] = (piece() * scale * gain_ref[:, cols]).astype(BF16)
        low_ref[...] = out_ref[:EDGE]
        high_ref[...] = out_ref[2 * TILE - EDGE :]


def attention(queries, key_value, low, high, edge, conv_gain):
    rows, width = queries.shape
    outs = []
    start = 0
    for g, pairs in enumerate(GROUPS):
        last = g == len(GROUPS) - 1
        base = [
            pl.BlockSpec(memory_space=pltpu.SMEM),
            pl.BlockSpec((rows, BLOCK), lambda j, s=start // SIDE: (0, s + j)),
            pl.BlockSpec((2, rows, BLOCK), lambda j, s=start // SIDE: (0, 0, s + j)),
            pl.BlockSpec((2, rows, BLOCK), lambda j: (0, 0, j)),
            pl.BlockSpec((2, rows, BLOCK), lambda j: (0, 0, j)),
        ]
        scratch = [pltpu.VMEM((2, TILE, SPAN), F32)]
        cost = (pairs * 16 * rows * SPAN * PAIR, pairs * 7 * rows * PAIR * 2)
        before, after = low[g], high[g]
        if outs:
            before, after, _ = lax.optimization_barrier((before, after, outs[-1]))
        args = (edge, queries, key_value, before, after)
        if not last:
            outs.append(
                call(
                    attend_body,
                    jax.ShapeDtypeStruct((rows, pairs * PAIR), F32),
                    cost,
                    58,
                    grid=(pairs // SIDE,),
                    in_specs=base,
                    out_specs=pl.BlockSpec((rows, BLOCK), lambda j: (0, j)),
                    scratch_shapes=scratch,
                )(*args)
            )
        else:
            whole = lambda *shape: pl.BlockSpec(shape, lambda j: (0,) * len(shape))
            return call(
                functools.partial(attend_norm_body, GROUPS[:-1]),
                [
                    jax.ShapeDtypeStruct((rows, width), BF16),
                    jax.ShapeDtypeStruct((EDGE, width), BF16),
                    jax.ShapeDtypeStruct((EDGE, width), BF16),
                ],
                cost,
                20,
                grid=(pairs // SIDE,),
                in_specs=base + [whole(1, width)] + [whole(*o.shape) for o in outs],
                out_specs=[whole(rows, width), whole(EDGE, width), whole(EDGE, width)],
                scratch_shapes=scratch + [pltpu.VMEM((pairs, rows, PAIR), F32)],
            )(*args, conv_gain[None], *outs)
        start += pairs


def silu(v):
    half = 0.5 * v
    return half + half * jnp.tanh(half)


def conv_rows(source, taps, first, count):
    total = jnp.zeros((count, PAIR), F32)
    for k in range(taps.shape[0]):
        total = total + taps[k : k + 1] * source[first + k : first + k + count]
    return source[first + 15 : first + 15 + count] + silu(total)


def inner_conv_body(normed_ref, taps_ref, out_ref, wide):
    wide[...] = normed_ref[...].astype(F32)
    count = 32
    for t in range(0, out_ref.shape[0], count):
        out_ref[t : t + count] = conv_rows(wide, taps_ref, EDGE + t - 15, count).astype(BF16)


def inner_conv(normed, taps):
    rows, width = normed.shape
    inner = rows - 2 * EDGE
    return call(
        inner_conv_body,
        jax.ShapeDtypeStruct((inner, width), BF16),
        (62 * inner * width * 64, 4 * rows * width),
        16,
        grid=(width // PAIR,),
        in_specs=[
            pl.BlockSpec((rows, PAIR), lambda j: (0, j)),
            pl.BlockSpec((taps.shape[0], PAIR), lambda j: (0, j)),
        ],
        out_specs=pl.BlockSpec((inner, PAIR), lambda j: (0, j)),
        scratch_shapes=[pltpu.VMEM((rows, PAIR), F32)],
    )(normed, taps)


def dispatch_body(normed_ref, inner_ref, low_ref, high_ref, taps_ref, gain_ref, place_ref, *rest):
    mixed_ref, outs, (wide,) = rest[0], rest[1:-1], rest[-1:]
    rows, width = normed_ref.shape
    for c in range(width // PAIR):
        cols = slice(c * PAIR, (c + 1) * PAIR)
        wide[0, :EDGE] = low_ref[:, cols].astype(F32)
        wide[0, EDGE:] = normed_ref[: 2 * EDGE, cols].astype(F32)
        wide[1, : 2 * EDGE] = normed_ref[rows - 2 * EDGE :, cols].astype(F32)
        wide[1, 2 * EDGE :] = high_ref[:, cols].astype(F32)
        taps = taps_ref.at[:, cols]
        mixed_ref[:EDGE, cols] = conv_rows(wide.at[0], taps, 1, EDGE).astype(BF16)
        mixed_ref[rows - EDGE :, cols] = conv_rows(wide.at[1], taps, 1, EDGE).astype(BF16)
    mixed_ref[EDGE : rows - EDGE] = inner_ref[...]
    mixed = mixed_ref[...].astype(F32)
    scale = lax.rsqrt(jnp.mean(mixed * mixed, axis=1, keepdims=True) + 1e-6)
    expert_in = (mixed * scale * gain_ref[...]).astype(BF16)
    first = 0
    for out_ref in outs:
        copies, count, _ = out_ref.shape
        place = first + lax.broadcasted_iota(jnp.int32, (count, rows), 0)
        pick = jnp.where(place == place_ref[...], 1.0, 0.0).astype(BF16)
        sent = jnp.dot(pick, expert_in, preferred_element_type=F32).astype(BF16)
        for z in range(copies):
            out_ref[z] = sent
        first += count


def dispatch(normed, inner, low, high, taps, gain, place, counts, copies):
    rows, width = normed.shape
    return call(
        dispatch_body,
        [jax.ShapeDtypeStruct((rows, width), BF16)]
        + [jax.ShapeDtypeStruct((copies, count, width), BF16) for count in counts],
        (2 * sum(counts) * rows * width, 8 * rows * width),
        24,
        scratch_shapes=[pltpu.VMEM((2, 3 * EDGE, PAIR), F32)],
    )(normed, inner, low, high, taps, gain[None], place[None])


def combine_body(mixed_ref, gate_ref, place_ref, *rest):
    parts, out_ref = rest[:-1], rest[-1]
    rows = mixed_ref.shape[0]
    total = None
    first = 0
    for part in parts:
        count = part.shape[0]
        place = first + lax.broadcasted_iota(jnp.int32, (rows, count), 1)
        pick = jnp.where(place == place_ref[...], 1.0, 0.0).astype(BF16)
        got = jnp.dot(pick, part[...], preferred_element_type=F32)
        total = got if total is None else total + got
        first += count
    out_ref[...] = (mixed_ref[...].astype(F32) + gate_ref[...] * total).astype(BF16)


def combine(mixed, gate, place, parts):
    rows, width = mixed.shape
    block = 256
    column = lambda n: pl.BlockSpec((n, block), lambda j: (0, j))
    fixed = pl.BlockSpec((rows, 1), lambda j: (0, 0))
    return call(
        combine_body,
        jax.ShapeDtypeStruct((rows, width), BF16),
        (2 * sum(p.shape[0] for p in parts) * rows * width, 8 * rows * width),
        16,
        grid=(width // block,),
        in_specs=[column(rows), fixed, fixed] + [column(p.shape[0]) for p in parts],
        out_specs=column(rows),
    )(mixed, gate[:, None], place[:, None], *parts)


def by_expert(n, axis):
    slots = n // DEVICES
    shift = slots.bit_length() - 1
    row = lax.broadcasted_iota(jnp.int32, (2 * n, 2 * n), axis)
    e = jnp.where(row >= n, 1, 0)
    r = row - e * n
    place = ((r >> shift) << (shift + 1)) + (e << shift) + (r & (slots - 1))
    return jnp.where(place == lax.broadcasted_iota(jnp.int32, (2 * n, 2 * n), 1 - axis), 1.0, 0.0).astype(BF16)


def ffn_body(direct, me, arrived, w_in, w_out, *rest):
    if direct:
        keep, to_right, to_left, to_far, *scratch = rest
    else:
        keep, up, down, up2, down2, *scratch = rest
    rows_in, hidden, first, second, sems = scratch
    n = arrived.shape[1] // 2
    width = arrived.shape[2]
    units = hidden.shape[1]
    step = STEP
    copies = {}
    for e in range(2):
        for which, (weight, held) in enumerate(((w_in, first), (w_out, second))):
            for t in range(weight.shape[2] // step):
                cols = slice(t * step, (t + 1) * step)
                copies[e, which, t] = pltpu.make_async_copy(
                    weight.at[e, :, cols], held.at[e, t], sems.at[e, which, t]
                )
                copies[e, which, t].start()
    order = by_expert(n, 0)
    for k, off in enumerate((0, 3, 1, 2)):
        block = jnp.dot(order, arrived[(me[0] + off) % 4], preferred_element_type=F32).astype(BF16)
        rows_in[0, k * n : (k + 1) * n] = block[:n]
        rows_in[1, k * n : (k + 1) * n] = block[n:]
    for e in range(2):
        for t in range(units // step):
            copies[e, 0, t].wait()
            part = jnp.dot(rows_in[e], first[e, t], preferred_element_type=F32)
            hidden[:, t * step : (t + 1) * step] = silu(part).astype(BF16)
        for t in range(width // step):
            copies[e, 1, t].wait()
            cols = slice(t * step, (t + 1) * step)
            part = jnp.dot(hidden[...], second[e, t], preferred_element_type=F32).astype(BF16)
            keep[e, :, cols] = part[:n]
            if direct:
                to_left[e, :, cols] = part[n : 2 * n]
                to_right[e, :, cols] = part[2 * n : 3 * n]
                to_far[e, :, cols] = part[3 * n :]
            elif e == 0:
                down[1, :, cols] = part[n : 2 * n]
                up2[:, cols] = part[2 * n : 3 * n]
                up[0, :, cols] = part[3 * n :]
            else:
                down2[:, cols] = part[n : 2 * n]
                up[1, :, cols] = part[2 * n : 3 * n]
                down[0, :, cols] = part[3 * n :]


def ffn(direct, me, arrived, w_in, w_out):
    n = arrived.shape[1] // 2
    experts, width, units = w_in.shape
    pair = jax.ShapeDtypeStruct((2, n, width), BF16)
    single = jax.ShapeDtypeStruct((n, width), BF16)
    return call(
        functools.partial(ffn_body, direct),
        [pair] * 4 if direct else [pair, pair, pair, single, single],
        (experts * 4 * n * width * units * 4, 2 * experts * width * units * 2),
        42,
        in_specs=[
            pl.BlockSpec(memory_space=pltpu.SMEM),
            pl.BlockSpec(memory_space=pltpu.VMEM),
            pl.BlockSpec(memory_space=pl.ANY),
            pl.BlockSpec(memory_space=pl.ANY),
        ],
        scratch_shapes=[
            pltpu.VMEM((2, 4 * n, width), BF16),
            pltpu.VMEM((4 * n, units), BF16),
            pltpu.VMEM((2, units // STEP, width, STEP), BF16),
            pltpu.VMEM((2, width // STEP, units, STEP), BF16),
            pltpu.SemaphoreType.DMA((2, 2, max(units, width) // STEP)),
        ],
    )(me, arrived, w_in, w_out)


def home_body(terms, *refs):
    ins, out_ref = refs[:-1], refs[-1]
    sums = []
    for chosen in terms:
        values = [(ins[i][...] if lead is None else ins[i][lead]).astype(F32) for i, lead in chosen]
        sums.append(sum(values[1:], values[0]).astype(BF16))
    rows = jnp.concatenate(sums, axis=0)
    order = by_expert(rows.shape[0] // 2, 1)
    out_ref[...] = jnp.dot(order, rows, preferred_element_type=F32).astype(BF16)


def home(terms, *arrays):
    _, n, width = arrays[0].shape
    return call(
        functools.partial(home_body, terms),
        jax.ShapeDtypeStruct((2 * n, width), BF16),
        (8 * n * n * width, 16 * n * width),
        24,
    )(*arrays)


def on_device(
    queries,
    key_value,
    conv_kernel,
    conv_gain,
    ffn_gain,
    expert_gate,
    primary,
    secondary,
    overflow,
    slot,
    w_in,
    w_out,
):
    frame_rows, width = queries.shape
    time_count = lax.axis_size("tm")
    group_count = lax.axis_size("expert")
    devices = time_count * group_count
    index = lax.axis_index("tm") * group_count + lax.axis_index("expert")
    edge = jnp.stack([index == 0, index == devices - 1]).astype(jnp.int32)
    order = ("tm", "expert")
    onward = [(i, i + 1) for i in range(devices - 1)]
    back = [(i + 1, i) for i in range(devices - 1)]

    low, high = [], []
    start = 0
    source = key_value
    for pairs in GROUPS:
        part = lax.slice_in_dim(source, start * PAIR, (start + pairs) * PAIR, axis=2)
        low.append(lax.ppermute(part, order, onward))
        high.append(lax.ppermute(part, order, back))
        start += pairs
        source, _ = lax.optimization_barrier((key_value, part))
    normed, first_rows, last_rows = attention(queries, key_value, low, high, edge, conv_gain)

    before = lax.ppermute(last_rows, order, onward)
    after = lax.ppermute(first_rows, order, back)
    inner = inner_conv(normed, conv_kernel)

    local = w_in.shape[0]
    experts = local * time_count
    slots = max(2, 3 * frame_rows // (2 * experts))
    early = 2 * slots // 3
    sizes = (early, slots - early)
    served = jnp.where(overflow == 1, secondary, primary)
    place = jnp.where(
        slot < early,
        served * early + slot,
        experts * early + served * (slots - early) + slot - early,
    )
    mixed, *chunks = dispatch(
        normed, inner, before, after, conv_kernel, ffn_gain, place, [experts * c for c in sizes], group_count
    )

    up = [(i, (i + 1) % group_count) for i in range(group_count)]
    down = [((i + 1) % group_count, i) for i in range(group_count)]
    add = lambda *vs: sum(v.astype(F32) for v in vs).astype(BF16)

    def arrive(chunk, size):
        sent = chunk.reshape(devices, local * size, width)
        got = lax.all_to_all(sent, ("expert", "tm"), split_axis=0, concat_axis=0, tiled=True)
        return got.reshape(group_count, experts * size, width)

    def leave(summed, size):
        summed = summed.reshape(time_count, local * size, width)
        got = lax.all_to_all(summed, "tm", split_axis=0, concat_axis=0, tiled=True)
        return got.reshape(experts * size, width)

    after = lambda values, *others: lax.optimization_barrier((tuple(values), others))[0]
    me = lax.axis_index("expert").astype(jnp.int32)[None]
    across = [(i, (i + 2) % group_count) for i in range(group_count)]
    rows_a = arrive(chunks[0], sizes[0])
    rows_b = arrive(*after((chunks[1],), rows_a), sizes[1])
    keep_a, go_up_a, go_down_a, up2_a, down2_a = ffn(False, me, rows_a, w_in, w_out)
    below_a, above_a = lax.ppermute(go_up_a, "expert", up), lax.ppermute(go_down_a, "expert", down)
    (rows_b,) = after((rows_b,), keep_a)
    keep_b, to_right, to_left, to_far = ffn(True, me, rows_b, w_in, w_out)
    below_a, above_a = after((below_a, above_a), keep_b)
    up2_a, down2_a = add(up2_a, below_a[0]), add(down2_a, above_a[0])
    up3_a, down3_a = lax.ppermute(up2_a, "expert", up), lax.ppermute(down2_a, "expert", down)
    to_right, to_left, to_far = after((to_right, to_left, to_far), up3_a, down3_a)
    parts_b = (
        lax.ppermute(to_right, "expert", up),
        lax.ppermute(to_left, "expert", down),
        lax.ppermute(to_far, "expert", across),
    )
    terms = (((0, 0), (1, 1), (3, None)), ((0, 1), (2, 1), (4, None)))
    total_a = home(terms, keep_a, above_a, below_a, up3_a, down3_a)
    back_a = leave(total_a, sizes[0])
    parts_b = after(parts_b, back_a)
    total_b = home([[(i, e) for i in range(4)] for e in range(2)], keep_b, *parts_b)
    back_b = leave(total_b, sizes[1])
    return combine(mixed, expert_gate, place, [back_a, back_b])


def solution(mesh):
    in_specs = (
        P(("tm", "expert"), None),
        P(None, ("tm", "expert"), None),
        P(),
        P(),
        P(),
        P(("tm", "expert")),
        P(("tm", "expert")),
        P(("tm", "expert")),
        P(("tm", "expert")),
        P(("tm", "expert")),
        P("tm", None, "expert"),
        P("tm", "expert", None),
    )
    out_specs = P(("tm", "expert"), None)
    return jax.shard_map(
        on_device, mesh=mesh, in_specs=in_specs, out_specs=out_specs, check_vma=False
    )
```

```python
import functools

import jax
import jax.numpy as jnp
from jax import lax
from jax.experimental import pallas as pl
from jax.experimental.pallas import tpu as pltpu
from jax.sharding import PartitionSpec as P

HEAD = 64
PAIR = 2 * HEAD
HALF = 256
TILE = 128
SPAN = 2 * HALF + TILE
EDGE = 16
GROUPS = (8, 4)
SIDE = 2
BLOCK = SIDE * PAIR
MIB = 1024 * 1024
STEP = 512
DEVICES = 32
F32 = jnp.float32
BF16 = jnp.bfloat16


def call(body, out_shape, cost, vmem, **kw):
    flops, moved = cost
    return pl.pallas_call(
        body,
        out_shape=out_shape,
        cost_estimate=pl.CostEstimate(flops=flops, bytes_accessed=moved, transcendentals=0),
        compiler_params=pltpu.CompilerParams(vmem_limit_bytes=vmem * MIB),
        **kw,
    )


def fill_bias(edge_ref, bias):
    @pl.when(pl.program_id(0) == 0)
    def _():
        row = lax.broadcasted_iota(jnp.int32, (TILE, SPAN), 0)
        col = lax.broadcasted_iota(jnp.int32, (TILE, SPAN), 1)
        for r in range(2):
            low = jnp.where(edge_ref[0] == 1, HALF - TILE * r, 0)
            high = jnp.where(edge_ref[1] == 1, 2 * HALF - TILE * r, SPAN)
            kept = (col > row) & (col - row < 2 * HALF) & (col >= low) & (col < high)
            bias[r] = jnp.where(kept, 0.0, -1e30)


def attend_pairs(q_ref, kv_ref, lo_ref, hi_ref, bias, put):
    lane = lax.broadcasted_iota(jnp.int32, (1, PAIR), 1)
    first = lane < HEAD
    only0 = jnp.where(first, 0.125, 0.0).astype(BF16)
    only1 = jnp.where(first, 0.0, 0.125).astype(BF16)
    ones = jnp.ones((SPAN, PAIR), BF16)
    for c in range(SIDE):
        cols = slice(c * PAIR, (c + 1) * PAIR)
        for r in range(2):
            if r == 0:
                join = lambda i: [lo_ref[i, :, cols], kv_ref[i, :, cols], hi_ref[i, :TILE, cols]]
            else:
                join = lambda i: [lo_ref[i, TILE:, cols], kv_ref[i, :, cols], hi_ref[i, :, cols]]
            rows = slice(r * TILE, (r + 1) * TILE)
            q = q_ref[rows, cols]
            both = jnp.concatenate([q * only0, q * only1], axis=0)
            s = lax.dot_general(
                both,
                jnp.concatenate(join(0), axis=0),
                (((1,), (1,)), ((), ())),
                preferred_element_type=F32,
            )
            s = s + jnp.concatenate([bias[r], bias[r]], axis=0)
            p = jnp.exp(s - jnp.max(s, axis=1, keepdims=True)).astype(BF16)
            values = jnp.concatenate([jnp.concatenate(join(1), axis=0), ones], axis=1)
            o = jnp.dot(p, values, preferred_element_type=F32)
            o = o[:, :PAIR] / o[:, PAIR:]
            put(c, rows, jnp.where(first, o[:TILE], o[TILE:]))


def attend_body(edge_ref, q_ref, kv_ref, lo_ref, hi_ref, out_ref, bias):
    fill_bias(edge_ref, bias)

    def put(c, rows, value):
        out_ref[rows, c * PAIR : (c + 1) * PAIR] = value

    attend_pairs(q_ref, kv_ref, lo_ref, hi_ref, bias, put)


def attend_norm_body(groups, edge_ref, q_ref, kv_ref, lo_ref, hi_ref, gain_ref, *rest):
    n = len(groups)
    earlier, (out_ref, low_ref, high_ref, bias, mine) = rest[:n], rest[n:]
    step = pl.program_id(0)
    fill_bias(edge_ref, bias)

    def put(c, rows, value):
        mine[step * SIDE + c, rows] = value

    attend_pairs(q_ref, kv_ref, lo_ref, hi_ref, bias, put)

    @pl.when(step == pl.num_programs(0) - 1)
    def _():
        blocks = [(ref, c) for ref, g in zip(earlier, groups) for c in range(g)]
        pieces = [(lambda ref=ref, c=c: ref[:, c * PAIR : (c + 1) * PAIR]) for ref, c in blocks]
        pieces += [(lambda c=c: mine[c]) for c in range(mine.shape[0])]
        total = jnp.zeros((2 * TILE, PAIR), F32)
        for piece in pieces:
            v = piece()
            total = total + v * v
        width = len(pieces) * PAIR
        scale = lax.rsqrt(jnp.sum(total, axis=1, keepdims=True) * (1.0 / width) + 1e-6)
        for c, piece in enumerate(pieces):
            cols = slice(c * PAIR, (c + 1) * PAIR)
            out_ref[:, cols] = (piece() * scale * gain_ref[:, cols]).astype(BF16)
        low_ref[...] = out_ref[:EDGE]
        high_ref[...] = out_ref[2 * TILE - EDGE :]


def attention(queries, key_value, low, high, edge, conv_gain):
    rows, width = queries.shape
    outs = []
    start = 0
    for g, pairs in enumerate(GROUPS):
        last = g == len(GROUPS) - 1
        base = [
            pl.BlockSpec(memory_space=pltpu.SMEM),
            pl.BlockSpec((rows, BLOCK), lambda j, s=start // SIDE: (0, s + j)),
            pl.BlockSpec((2, rows, BLOCK), lambda j, s=start // SIDE: (0, 0, s + j)),
            pl.BlockSpec((2, rows, BLOCK), lambda j: (0, 0, j)),
            pl.BlockSpec((2, rows, BLOCK), lambda j: (0, 0, j)),
        ]
        scratch = [pltpu.VMEM((2, TILE, SPAN), F32)]
        cost = (pairs * 16 * rows * SPAN * PAIR, pairs * 7 * rows * PAIR * 2)
        before, after = low[g], high[g]
        if outs:
            before, after, _ = lax.optimization_barrier((before, after, outs[-1]))
        args = (edge, queries, key_value, before, after)
        if not last:
            outs.append(
                call(
                    attend_body,
                    jax.ShapeDtypeStruct((rows, pairs * PAIR), F32),
                    cost,
                    58,
                    grid=(pairs // SIDE,),
                    in_specs=base,
                    out_specs=pl.BlockSpec((rows, BLOCK), lambda j: (0, j)),
                    scratch_shapes=scratch,
                )(*args)
            )
        else:
            whole = lambda *shape: pl.BlockSpec(shape, lambda j: (0,) * len(shape))
            return call(
                functools.partial(attend_norm_body, GROUPS[:-1]),
                [
                    jax.ShapeDtypeStruct((rows, width), BF16),
                    jax.ShapeDtypeStruct((EDGE, width), BF16),
                    jax.ShapeDtypeStruct((EDGE, width), BF16),
                ],
                cost,
                20,
                grid=(pairs // SIDE,),
                in_specs=base + [whole(1, width)] + [whole(*o.shape) for o in outs],
                out_specs=[whole(rows, width), whole(EDGE, width), whole(EDGE, width)],
                scratch_shapes=scratch + [pltpu.VMEM((pairs, rows, PAIR), F32)],
            )(*args, conv_gain[None], *outs)
        start += pairs


def silu(v):
    half = 0.5 * v
    return half + half * jnp.tanh(half)


def conv_rows(source, taps, first, count):
    total = jnp.zeros((count, PAIR), F32)
    for k in range(taps.shape[0]):
        total = total + taps[k : k + 1] * source[first + k : first + k + count]
    return source[first + 15 : first + 15 + count] + silu(total)


def inner_conv_body(normed_ref, taps_ref, out_ref, wide):
    wide[...] = normed_ref[...].astype(F32)
    count = 32
    for t in range(0, out_ref.shape[0], count):
        out_ref[t : t + count] = conv_rows(wide, taps_ref, EDGE + t - 15, count).astype(BF16)


def inner_conv(normed, taps):
    rows, width = normed.shape
    inner = rows - 2 * EDGE
    return call(
        inner_conv_body,
        jax.ShapeDtypeStruct((inner, width), BF16),
        (62 * inner * width * 64, 4 * rows * width),
        16,
        grid=(width // PAIR,),
        in_specs=[
            pl.BlockSpec((rows, PAIR), lambda j: (0, j)),
            pl.BlockSpec((taps.shape[0], PAIR), lambda j: (0, j)),
        ],
        out_specs=pl.BlockSpec((inner, PAIR), lambda j: (0, j)),
        scratch_shapes=[pltpu.VMEM((rows, PAIR), F32)],
    )(normed, taps)


def dispatch_body(normed_ref, inner_ref, low_ref, high_ref, taps_ref, gain_ref, place_ref, *rest):
    mixed_ref, outs, (wide,) = rest[0], rest[1:-1], rest[-1:]
    rows, width = normed_ref.shape
    for c in range(width // PAIR):
        cols = slice(c * PAIR, (c + 1) * PAIR)
        wide[0, :EDGE] = low_ref[:, cols].astype(F32)
        wide[0, EDGE:] = normed_ref[: 2 * EDGE, cols].astype(F32)
        wide[1, : 2 * EDGE] = normed_ref[rows - 2 * EDGE :, cols].astype(F32)
        wide[1, 2 * EDGE :] = high_ref[:, cols].astype(F32)
        taps = taps_ref.at[:, cols]
        mixed_ref[:EDGE, cols] = conv_rows(wide.at[0], taps, 1, EDGE).astype(BF16)
        mixed_ref[rows - EDGE :, cols] = conv_rows(wide.at[1], taps, 1, EDGE).astype(BF16)
    mixed_ref[EDGE : rows - EDGE] = inner_ref[...]
    mixed = mixed_ref[...].astype(F32)
    scale = lax.rsqrt(jnp.mean(mixed * mixed, axis=1, keepdims=True) + 1e-6)
    expert_in = (mixed * scale * gain_ref[...]).astype(BF16)
    first = 0
    for out_ref in outs:
        count = out_ref.shape[0]
        place = first + lax.broadcasted_iota(jnp.int32, (count, rows), 0)
        pick = jnp.where(place == place_ref[...], 1.0, 0.0).astype(BF16)
        out_ref[...] = jnp.dot(pick, expert_in, preferred_element_type=F32).astype(BF16)
        first += count


def dispatch(normed, inner, low, high, taps, gain, place, counts):
    rows, width = normed.shape
    return call(
        dispatch_body,
        [jax.ShapeDtypeStruct((rows, width), BF16)]
        + [jax.ShapeDtypeStruct((count, width), BF16) for count in counts],
        (2 * sum(counts) * rows * width, 8 * rows * width),
        24,
        scratch_shapes=[pltpu.VMEM((2, 3 * EDGE, PAIR), F32)],
    )(normed, inner, low, high, taps, gain[None], place[None])


def combine_body(mixed_ref, gate_ref, place_ref, *rest):
    parts, out_ref = rest[:-1], rest[-1]
    rows = mixed_ref.shape[0]
    total = None
    first = 0
    for part in parts:
        count = part.shape[0]
        place = first + lax.broadcasted_iota(jnp.int32, (rows, count), 1)
        pick = jnp.where(place == place_ref[...], 1.0, 0.0).astype(BF16)
        got = jnp.dot(pick, part[...], preferred_element_type=F32)
        total = got if total is None else total + got
        first += count
    out_ref[...] = (mixed_ref[...].astype(F32) + gate_ref[...] * total).astype(BF16)


def combine(mixed, gate, place, parts):
    rows, width = mixed.shape
    block = 256
    column = lambda n: pl.BlockSpec((n, block), lambda j: (0, j))
    fixed = pl.BlockSpec((rows, 1), lambda j: (0, 0))
    return call(
        combine_body,
        jax.ShapeDtypeStruct((rows, width), BF16),
        (2 * sum(p.shape[0] for p in parts) * rows * width, 8 * rows * width),
        16,
        grid=(width // block,),
        in_specs=[column(rows), fixed, fixed] + [column(p.shape[0]) for p in parts],
        out_specs=column(rows),
    )(mixed, gate[:, None], place[:, None], *parts)


def by_expert(n, axis):
    slots = n // DEVICES
    row = lax.broadcasted_iota(jnp.int32, (2 * n, 2 * n), axis)
    e = jnp.where(row >= n, 1, 0)
    r = row - e * n
    device = (r * (4096 // slots + 1)) >> 12
    place = device * slots + e * slots + r
    return jnp.where(place == lax.broadcasted_iota(jnp.int32, (2 * n, 2 * n), 1 - axis), 1.0, 0.0).astype(BF16)


def ffn_body(direct, own, left, right, *rest):
    far, (w_in, w_out, *rest) = (rest[:1], rest[1:]) if direct else (rest[:2], rest[2:])
    if direct:
        keep, to_right, to_left, to_far, *scratch = rest
    else:
        keep, up, down, up2, down2, *scratch = rest
    rows_in, hidden, first, second, sems = scratch
    n = own.shape[0] // 2
    width = own.shape[1]
    units = hidden.shape[1]
    step = STEP
    copies = {}
    for e in range(2):
        for which, (weight, held) in enumerate(((w_in, first), (w_out, second))):
            for t in range(weight.shape[2] // step):
                cols = slice(t * step, (t + 1) * step)
                copies[e, which, t] = pltpu.make_async_copy(
                    weight.at[e, :, cols], held.at[e, t], sems.at[e, which, t]
                )
                copies[e, which, t].start()
    order = by_expert(n, 0)
    for k, refs in enumerate(((own,), (left,), (right,), far)):
        block = jnp.concatenate([ref[...] for ref in refs], axis=0)
        block = jnp.dot(order, block, preferred_element_type=F32).astype(BF16)
        rows_in[0, k * n : (k + 1) * n] = block[:n]
        rows_in[1, k * n : (k + 1) * n] = block[n:]
    for e in range(2):
        for t in range(units // step):
            copies[e, 0, t].wait()
            part = jnp.dot(rows_in[e], first[e, t], preferred_element_type=F32)
            hidden[:, t * step : (t + 1) * step] = silu(part).astype(BF16)
        for t in range(width // step):
            copies[e, 1, t].wait()
            cols = slice(t * step, (t + 1) * step)
            part = jnp.dot(hidden[...], second[e, t], preferred_element_type=F32).astype(BF16)
            keep[e, :, cols] = part[:n]
            if direct:
                to_left[e, :, cols] = part[n : 2 * n]
                to_right[e, :, cols] = part[2 * n : 3 * n]
                to_far[e, :, cols] = part[3 * n :]
            elif e == 0:
                down[1, :, cols] = part[n : 2 * n]
                up2[:, cols] = part[2 * n : 3 * n]
                up[0, :, cols] = part[3 * n :]
            else:
                down2[:, cols] = part[n : 2 * n]
                up[1, :, cols] = part[2 * n : 3 * n]
                down[0, :, cols] = part[3 * n :]


def ffn(own, left, right, far, w_in, w_out):
    direct = len(far) == 1
    n = own.shape[0] // 2
    experts, width, units = w_in.shape
    pair = jax.ShapeDtypeStruct((2, n, width), BF16)
    single = jax.ShapeDtypeStruct((n, width), BF16)
    return call(
        functools.partial(ffn_body, direct),
        [pair] * 4 if direct else [pair, pair, pair, single, single],
        (experts * 4 * n * width * units * 4, 2 * experts * width * units * 2),
        42,
        in_specs=[
            *[pl.BlockSpec(memory_space=pltpu.VMEM)] * (3 + len(far)),
            pl.BlockSpec(memory_space=pl.ANY),
            pl.BlockSpec(memory_space=pl.ANY),
        ],
        scratch_shapes=[
            pltpu.VMEM((2, 4 * n, width), BF16),
            pltpu.VMEM((4 * n, units), BF16),
            pltpu.VMEM((2, units // STEP, width, STEP), BF16),
            pltpu.VMEM((2, width // STEP, units, STEP), BF16),
            pltpu.SemaphoreType.DMA((2, 2, max(units, width) // STEP)),
        ],
    )(own, left, right, *far, w_in, w_out)


def home_body(terms, *refs):
    ins, out_ref = refs[:-1], refs[-1]
    sums = []
    for chosen in terms:
        values = [(ins[i][...] if lead is None else ins[i][lead]).astype(F32) for i, lead in chosen]
        sums.append(sum(values[1:], values[0]).astype(BF16))
    rows = jnp.concatenate(sums, axis=0)
    order = by_expert(rows.shape[0] // 2, 1)
    out_ref[...] = jnp.dot(order, rows, preferred_element_type=F32).astype(BF16)


def home(terms, *arrays):
    _, n, width = arrays[0].shape
    return call(
        functools.partial(home_body, terms),
        jax.ShapeDtypeStruct((2 * n, width), BF16),
        (8 * n * n * width, 16 * n * width),
        24,
    )(*arrays)


def on_device(
    queries,
    key_value,
    conv_kernel,
    conv_gain,
    ffn_gain,
    expert_gate,
    primary,
    secondary,
    overflow,
    slot,
    w_in,
    w_out,
):
    frame_rows, width = queries.shape
    time_count = lax.axis_size("tm")
    group_count = lax.axis_size("expert")
    devices = time_count * group_count
    index = lax.axis_index("tm") * group_count + lax.axis_index("expert")
    edge = jnp.stack([index == 0, index == devices - 1]).astype(jnp.int32)
    order = ("tm", "expert")
    onward = [(i, i + 1) for i in range(devices - 1)]
    back = [(i + 1, i) for i in range(devices - 1)]

    low, high = [], []
    start = 0
    source = key_value
    for pairs in GROUPS:
        part = lax.slice_in_dim(source, start * PAIR, (start + pairs) * PAIR, axis=2)
        low.append(lax.ppermute(part, order, onward))
        high.append(lax.ppermute(part, order, back))
        start += pairs
        source, _ = lax.optimization_barrier((key_value, part))
    normed, first_rows, last_rows = attention(queries, key_value, low, high, edge, conv_gain)

    before = lax.ppermute(last_rows, order, onward)
    after = lax.ppermute(first_rows, order, back)
    inner = inner_conv(normed, conv_kernel)

    local = w_in.shape[0]
    experts = local * time_count
    slots = max(2, 3 * frame_rows // (2 * experts))
    early = slots // 2
    sizes = (early, slots - early)
    served = jnp.where(overflow == 1, secondary, primary)
    place = jnp.where(
        slot < early,
        served * early + slot,
        experts * early + served * (slots - early) + slot - early,
    )
    mixed, *chunks = dispatch(
        normed, inner, before, after, conv_kernel, ffn_gain, place, [experts * c for c in sizes]
    )

    up = [(i, (i + 1) % group_count) for i in range(group_count)]
    down = [((i + 1) % group_count, i) for i in range(group_count)]
    add = lambda *vs: sum(v.astype(F32) for v in vs).astype(BF16)

    def arrive(chunk, size):
        sent = chunk.reshape(time_count, local * size, width)
        got = lax.all_to_all(sent, "tm", split_axis=0, concat_axis=0, tiled=True)
        return got.reshape(experts * size, width)

    def near(own):
        return lax.ppermute(own, "expert", up), lax.ppermute(own, "expert", down)

    def leave(summed, size):
        summed = summed.reshape(time_count, local * size, width)
        got = lax.all_to_all(summed, "tm", split_axis=0, concat_axis=0, tiled=True)
        return got.reshape(experts * size, width)

    after = lambda values, *others: lax.optimization_barrier((tuple(values), others))[0]
    across = [(i, (i + 2) % group_count) for i in range(group_count)]
    own_a = arrive(chunks[0], sizes[0])
    left_a, right_a = near(own_a)
    own_b = arrive(*after((chunks[1],), own_a), sizes[1])
    left_a, right_a = after((left_a, right_a), own_b)
    half = own_a.shape[0] // 2
    far_a = lax.ppermute(left_a[:half], "expert", up), lax.ppermute(right_a[half:], "expert", down)
    left_b, right_b = near(own_b)
    far_b = lax.ppermute(own_b, "expert", across)
    keep_a, go_up_a, go_down_a, up2_a, down2_a = ffn(own_a, left_a, right_a, far_a, w_in, w_out)
    below_a, above_a = lax.ppermute(go_up_a, "expert", up), lax.ppermute(go_down_a, "expert", down)
    (own_b,) = after((own_b,), keep_a)
    keep_b, to_right, to_left, to_far = ffn(own_b, left_b, right_b, (far_b,), w_in, w_out)
    below_a, above_a = after((below_a, above_a), keep_b)
    up2_a, down2_a = add(up2_a, below_a[0]), add(down2_a, above_a[0])
    up3_a, down3_a = lax.ppermute(up2_a, "expert", up), lax.ppermute(down2_a, "expert", down)
    to_right, to_left, to_far = after((to_right, to_left, to_far), up3_a, down3_a)
    parts_b = (
        lax.ppermute(to_right, "expert", up),
        lax.ppermute(to_left, "expert", down),
        lax.ppermute(to_far, "expert", across),
    )
    terms = (((0, 0), (1, 1), (3, None)), ((0, 1), (2, 1), (4, None)))
    total_a = home(terms, keep_a, above_a, below_a, up3_a, down3_a)
    back_a = leave(total_a, sizes[0])
    parts_b = after(parts_b, back_a)
    total_b = home([[(i, e) for i in range(4)] for e in range(2)], keep_b, *parts_b)
    back_b = leave(total_b, sizes[1])
    return combine(mixed, expert_gate, place, [back_a, back_b])


def solution(mesh):
    in_specs = (
        P(("tm", "expert"), None),
        P(None, ("tm", "expert"), None),
        P(),
        P(),
        P(),
        P(("tm", "expert")),
        P(("tm", "expert")),
        P(("tm", "expert")),
        P(("tm", "expert")),
        P(("tm", "expert")),
        P("tm", None, "expert"),
        P("tm", "expert", None),
    )
    out_specs = P(("tm", "expert"), None)
    return jax.shard_map(
        on_device, mesh=mesh, in_specs=in_specs, out_specs=out_specs, check_vma=False
    )
```

```python
import functools

import jax
import jax.numpy as jnp
from jax import lax
from jax.experimental import pallas as pl
from jax.experimental.pallas import tpu as pltpu
from jax.sharding import PartitionSpec as P

HEAD = 64
PAIR = 2 * HEAD
HALF = 256
TILE = 128
SPAN = 2 * HALF + TILE
EDGE = 16
GROUPS = (8, 4)
SIDE = 2
BLOCK = SIDE * PAIR
MIB = 1024 * 1024
STEP = 512
DEVICES = 32
F32 = jnp.float32
BF16 = jnp.bfloat16


def call(body, out_shape, cost, vmem, **kw):
    flops, moved = cost
    return pl.pallas_call(
        body,
        out_shape=out_shape,
        cost_estimate=pl.CostEstimate(flops=flops, bytes_accessed=moved, transcendentals=0),
        compiler_params=pltpu.CompilerParams(vmem_limit_bytes=vmem * MIB),
        **kw,
    )


def fill_bias(edge_ref, bias):
    @pl.when(pl.program_id(0) == 0)
    def _():
        row = lax.broadcasted_iota(jnp.int32, (TILE, SPAN), 0)
        col = lax.broadcasted_iota(jnp.int32, (TILE, SPAN), 1)
        for r in range(2):
            low = jnp.where(edge_ref[0] == 1, HALF - TILE * r, 0)
            high = jnp.where(edge_ref[1] == 1, 2 * HALF - TILE * r, SPAN)
            kept = (col > row) & (col - row < 2 * HALF) & (col >= low) & (col < high)
            bias[r] = jnp.where(kept, 0.0, -1e30)


def attend_pairs(q_ref, kv_ref, lo_ref, hi_ref, bias, put):
    lane = lax.broadcasted_iota(jnp.int32, (1, PAIR), 1)
    first = lane < HEAD
    only0 = jnp.where(first, 0.125, 0.0).astype(BF16)
    only1 = jnp.where(first, 0.0, 0.125).astype(BF16)
    ones = jnp.ones((SPAN, PAIR), BF16)
    for c in range(SIDE):
        cols = slice(c * PAIR, (c + 1) * PAIR)
        for r in range(2):
            if r == 0:
                join = lambda i: [lo_ref[i, :, cols], kv_ref[i, :, cols], hi_ref[i, :TILE, cols]]
            else:
                join = lambda i: [lo_ref[i, TILE:, cols], kv_ref[i, :, cols], hi_ref[i, :, cols]]
            rows = slice(r * TILE, (r + 1) * TILE)
            q = q_ref[rows, cols]
            both = jnp.concatenate([q * only0, q * only1], axis=0)
            s = lax.dot_general(
                both,
                jnp.concatenate(join(0), axis=0),
                (((1,), (1,)), ((), ())),
                preferred_element_type=F32,
            )
            s = s + jnp.concatenate([bias[r], bias[r]], axis=0)
            p = jnp.exp(s - jnp.max(s, axis=1, keepdims=True)).astype(BF16)
            values = jnp.concatenate([jnp.concatenate(join(1), axis=0), ones], axis=1)
            o = jnp.dot(p, values, preferred_element_type=F32)
            o = o[:, :PAIR] / o[:, PAIR:]
            put(c, rows, jnp.where(first, o[:TILE], o[TILE:]))


def attend_body(edge_ref, q_ref, kv_ref, lo_ref, hi_ref, out_ref, bias):
    fill_bias(edge_ref, bias)

    def put(c, rows, value):
        out_ref[rows, c * PAIR : (c + 1) * PAIR] = value

    attend_pairs(q_ref, kv_ref, lo_ref, hi_ref, bias, put)


def attend_norm_body(groups, edge_ref, q_ref, kv_ref, lo_ref, hi_ref, gain_ref, *rest):
    n = len(groups)
    earlier, (out_ref, low_ref, high_ref, bias, mine) = rest[:n], rest[n:]
    step = pl.program_id(0)
    fill_bias(edge_ref, bias)

    def put(c, rows, value):
        mine[step * SIDE + c, rows] = value

    attend_pairs(q_ref, kv_ref, lo_ref, hi_ref, bias, put)

    @pl.when(step == pl.num_programs(0) - 1)
    def _():
        blocks = [(ref, c) for ref, g in zip(earlier, groups) for c in range(g)]
        pieces = [(lambda ref=ref, c=c: ref[:, c * PAIR : (c + 1) * PAIR]) for ref, c in blocks]
        pieces += [(lambda c=c: mine[c]) for c in range(mine.shape[0])]
        total = jnp.zeros((2 * TILE, PAIR), F32)
        for piece in pieces:
            v = piece()
            total = total + v * v
        width = len(pieces) * PAIR
        scale = lax.rsqrt(jnp.sum(total, axis=1, keepdims=True) * (1.0 / width) + 1e-6)
        for c, piece in enumerate(pieces):
            cols = slice(c * PAIR, (c + 1) * PAIR)
            out_ref[:, cols] = (piece() * scale * gain_ref[:, cols]).astype(BF16)
        low_ref[...] = out_ref[:EDGE]
        high_ref[...] = out_ref[2 * TILE - EDGE :]


def attention(queries, key_value, low, high, edge, conv_gain):
    rows, width = queries.shape
    outs = []
    start = 0
    for g, pairs in enumerate(GROUPS):
        last = g == len(GROUPS) - 1
        base = [
            pl.BlockSpec(memory_space=pltpu.SMEM),
            pl.BlockSpec((rows, BLOCK), lambda j, s=start // SIDE: (0, s + j)),
            pl.BlockSpec((2, rows, BLOCK), lambda j, s=start // SIDE: (0, 0, s + j)),
            pl.BlockSpec((2, rows, BLOCK), lambda j: (0, 0, j)),
            pl.BlockSpec((2, rows, BLOCK), lambda j: (0, 0, j)),
        ]
        scratch = [pltpu.VMEM((2, TILE, SPAN), F32)]
        cost = (pairs * 16 * rows * SPAN * PAIR, pairs * 7 * rows * PAIR * 2)
        before, after = low[g], high[g]
        if outs:
            before, after, _ = lax.optimization_barrier((before, after, outs[-1]))
        args = (edge, queries, key_value, before, after)
        if not last:
            outs.append(
                call(
                    attend_body,
                    jax.ShapeDtypeStruct((rows, pairs * PAIR), F32),
                    cost,
                    58,
                    grid=(pairs // SIDE,),
                    in_specs=base,
                    out_specs=pl.BlockSpec((rows, BLOCK), lambda j: (0, j)),
                    scratch_shapes=scratch,
                )(*args)
            )
        else:
            whole = lambda *shape: pl.BlockSpec(shape, lambda j: (0,) * len(shape))
            return call(
                functools.partial(attend_norm_body, GROUPS[:-1]),
                [
                    jax.ShapeDtypeStruct((rows, width), BF16),
                    jax.ShapeDtypeStruct((EDGE, width), BF16),
                    jax.ShapeDtypeStruct((EDGE, width), BF16),
                ],
                cost,
                20,
                grid=(pairs // SIDE,),
                in_specs=base + [whole(1, width)] + [whole(*o.shape) for o in outs],
                out_specs=[whole(rows, width), whole(EDGE, width), whole(EDGE, width)],
                scratch_shapes=scratch + [pltpu.VMEM((pairs, rows, PAIR), F32)],
            )(*args, conv_gain[None], *outs)
        start += pairs


def silu(v):
    half = 0.5 * v
    return half + half * jnp.tanh(half)


def conv_rows(source, taps, first, count):
    total = jnp.zeros((count, PAIR), F32)
    for k in range(taps.shape[0]):
        total = total + taps[k : k + 1] * source[first + k : first + k + count]
    return source[first + 15 : first + 15 + count] + silu(total)


def inner_conv_body(normed_ref, taps_ref, out_ref, wide):
    wide[...] = normed_ref[...].astype(F32)
    count = 32
    for t in range(0, out_ref.shape[0], count):
        out_ref[t : t + count] = conv_rows(wide, taps_ref, EDGE + t - 15, count).astype(BF16)


def inner_conv(normed, taps):
    rows, width = normed.shape
    inner = rows - 2 * EDGE
    return call(
        inner_conv_body,
        jax.ShapeDtypeStruct((inner, width), BF16),
        (62 * inner * width * 64, 4 * rows * width),
        16,
        grid=(width // PAIR,),
        in_specs=[
            pl.BlockSpec((rows, PAIR), lambda j: (0, j)),
            pl.BlockSpec((taps.shape[0], PAIR), lambda j: (0, j)),
        ],
        out_specs=pl.BlockSpec((inner, PAIR), lambda j: (0, j)),
        scratch_shapes=[pltpu.VMEM((rows, PAIR), F32)],
    )(normed, taps)


def dispatch_body(normed_ref, inner_ref, low_ref, high_ref, taps_ref, gain_ref, place_ref, *rest):
    mixed_ref, outs, (wide,) = rest[0], rest[1:-1], rest[-1:]
    rows, width = normed_ref.shape
    for c in range(width // PAIR):
        cols = slice(c * PAIR, (c + 1) * PAIR)
        wide[0, :EDGE] = low_ref[:, cols].astype(F32)
        wide[0, EDGE:] = normed_ref[: 2 * EDGE, cols].astype(F32)
        wide[1, : 2 * EDGE] = normed_ref[rows - 2 * EDGE :, cols].astype(F32)
        wide[1, 2 * EDGE :] = high_ref[:, cols].astype(F32)
        taps = taps_ref.at[:, cols]
        mixed_ref[:EDGE, cols] = conv_rows(wide.at[0], taps, 1, EDGE).astype(BF16)
        mixed_ref[rows - EDGE :, cols] = conv_rows(wide.at[1], taps, 1, EDGE).astype(BF16)
    mixed_ref[EDGE : rows - EDGE] = inner_ref[...]
    mixed = mixed_ref[...].astype(F32)
    scale = lax.rsqrt(jnp.mean(mixed * mixed, axis=1, keepdims=True) + 1e-6)
    expert_in = (mixed * scale * gain_ref[...]).astype(BF16)
    first = 0
    for out_ref in outs:
        count = out_ref.shape[0]
        place = first + lax.broadcasted_iota(jnp.int32, (count, rows), 0)
        pick = jnp.where(place == place_ref[...], 1.0, 0.0).astype(BF16)
        out_ref[...] = jnp.dot(pick, expert_in, preferred_element_type=F32).astype(BF16)
        first += count


def dispatch(normed, inner, low, high, taps, gain, place, counts):
    rows, width = normed.shape
    return call(
        dispatch_body,
        [jax.ShapeDtypeStruct((rows, width), BF16)]
        + [jax.ShapeDtypeStruct((count, width), BF16) for count in counts],
        (2 * sum(counts) * rows * width, 8 * rows * width),
        24,
        scratch_shapes=[pltpu.VMEM((2, 3 * EDGE, PAIR), F32)],
    )(normed, inner, low, high, taps, gain[None], place[None])


def combine_body(mixed_ref, gate_ref, place_ref, *rest):
    parts, out_ref = rest[:-1], rest[-1]
    rows = mixed_ref.shape[0]
    total = None
    first = 0
    for part in parts:
        count = part.shape[0]
        place = first + lax.broadcasted_iota(jnp.int32, (rows, count), 1)
        pick = jnp.where(place == place_ref[...], 1.0, 0.0).astype(BF16)
        got = jnp.dot(pick, part[...], preferred_element_type=F32)
        total = got if total is None else total + got
        first += count
    out_ref[...] = (mixed_ref[...].astype(F32) + gate_ref[...] * total).astype(BF16)


def combine(mixed, gate, place, parts):
    rows, width = mixed.shape
    block = 256
    column = lambda n: pl.BlockSpec((n, block), lambda j: (0, j))
    fixed = pl.BlockSpec((rows, 1), lambda j: (0, 0))
    return call(
        combine_body,
        jax.ShapeDtypeStruct((rows, width), BF16),
        (2 * sum(p.shape[0] for p in parts) * rows * width, 8 * rows * width),
        16,
        grid=(width // block,),
        in_specs=[column(rows), fixed, fixed] + [column(p.shape[0]) for p in parts],
        out_specs=column(rows),
    )(mixed, gate[:, None], place[:, None], *parts)


def by_expert(n, axis):
    slots = n // DEVICES
    row = lax.broadcasted_iota(jnp.int32, (2 * n, 2 * n), axis)
    e = jnp.where(row >= n, 1, 0)
    r = row - e * n
    device = (r * (4096 // slots + 1)) >> 12
    place = device * slots + e * slots + r
    return jnp.where(place == lax.broadcasted_iota(jnp.int32, (2 * n, 2 * n), 1 - axis), 1.0, 0.0).astype(BF16)


def ffn_body(direct, own, left, right, *rest):
    far, (w_in, w_out, *rest) = (rest[:1], rest[1:]) if direct else (rest[:2], rest[2:])
    if direct:
        keep, to_right, to_left, to_far, *scratch = rest
    else:
        keep, up, down, up2, down2, *scratch = rest
    rows_in, hidden, first, second, sems = scratch
    n = own.shape[0] // 2
    width = own.shape[1]
    units = hidden.shape[1]
    step = STEP
    copies = {}
    for e in range(2):
        for which, (weight, held) in enumerate(((w_in, first), (w_out, second))):
            for t in range(weight.shape[2] // step):
                cols = slice(t * step, (t + 1) * step)
                copies[e, which, t] = pltpu.make_async_copy(
                    weight.at[e, :, cols], held.at[e, t], sems.at[e, which, t]
                )
                copies[e, which, t].start()
    order = by_expert(n, 0)
    for k, refs in enumerate(((own,), (left,), (right,), far)):
        block = jnp.concatenate([ref[...] for ref in refs], axis=0)
        block = jnp.dot(order, block, preferred_element_type=F32).astype(BF16)
        rows_in[0, k * n : (k + 1) * n] = block[:n]
        rows_in[1, k * n : (k + 1) * n] = block[n:]
    for e in range(2):
        for t in range(units // step):
            copies[e, 0, t].wait()
            part = jnp.dot(rows_in[e], first[e, t], preferred_element_type=F32)
            hidden[:, t * step : (t + 1) * step] = silu(part).astype(BF16)
        for t in range(width // step):
            copies[e, 1, t].wait()
            cols = slice(t * step, (t + 1) * step)
            part = jnp.dot(hidden[...], second[e, t], preferred_element_type=F32).astype(BF16)
            keep[e, :, cols] = part[:n]
            if direct:
                to_left[e, :, cols] = part[n : 2 * n]
                to_right[e, :, cols] = part[2 * n : 3 * n]
                to_far[e, :, cols] = part[3 * n :]
            elif e == 0:
                down[1, :, cols] = part[n : 2 * n]
                up2[:, cols] = part[2 * n : 3 * n]
                up[0, :, cols] = part[3 * n :]
            else:
                down2[:, cols] = part[n : 2 * n]
                up[1, :, cols] = part[2 * n : 3 * n]
                down[0, :, cols] = part[3 * n :]


def ffn(own, left, right, far, w_in, w_out):
    direct = len(far) == 1
    n = own.shape[0] // 2
    experts, width, units = w_in.shape
    pair = jax.ShapeDtypeStruct((2, n, width), BF16)
    single = jax.ShapeDtypeStruct((n, width), BF16)
    return call(
        functools.partial(ffn_body, direct),
        [pair] * 4 if direct else [pair, pair, pair, single, single],
        (experts * 4 * n * width * units * 4, 2 * experts * width * units * 2),
        42,
        in_specs=[
            *[pl.BlockSpec(memory_space=pltpu.VMEM)] * (3 + len(far)),
            pl.BlockSpec(memory_space=pl.ANY),
            pl.BlockSpec(memory_space=pl.ANY),
        ],
        scratch_shapes=[
            pltpu.VMEM((2, 4 * n, width), BF16),
            pltpu.VMEM((4 * n, units), BF16),
            pltpu.VMEM((2, units // STEP, width, STEP), BF16),
            pltpu.VMEM((2, width // STEP, units, STEP), BF16),
            pltpu.SemaphoreType.DMA((2, 2, max(units, width) // STEP)),
        ],
    )(own, left, right, *far, w_in, w_out)


def home_body(terms, *refs):
    ins, out_ref = refs[:-1], refs[-1]
    sums = []
    for chosen in terms:
        values = [(ins[i][...] if lead is None else ins[i][lead]).astype(F32) for i, lead in chosen]
        sums.append(sum(values[1:], values[0]).astype(BF16))
    rows = jnp.concatenate(sums, axis=0)
    order = by_expert(rows.shape[0] // 2, 1)
    out_ref[...] = jnp.dot(order, rows, preferred_element_type=F32).astype(BF16)


def home(terms, *arrays):
    _, n, width = arrays[0].shape
    return call(
        functools.partial(home_body, terms),
        jax.ShapeDtypeStruct((2 * n, width), BF16),
        (8 * n * n * width, 16 * n * width),
        24,
    )(*arrays)


def on_device(
    queries,
    key_value,
    conv_kernel,
    conv_gain,
    ffn_gain,
    expert_gate,
    primary,
    secondary,
    overflow,
    slot,
    w_in,
    w_out,
):
    frame_rows, width = queries.shape
    time_count = lax.axis_size("tm")
    group_count = lax.axis_size("expert")
    devices = time_count * group_count
    index = lax.axis_index("tm") * group_count + lax.axis_index("expert")
    edge = jnp.stack([index == 0, index == devices - 1]).astype(jnp.int32)
    order = ("tm", "expert")
    onward = [(i, i + 1) for i in range(devices - 1)]
    back = [(i + 1, i) for i in range(devices - 1)]

    low, high = [], []
    start = 0
    source = key_value
    for pairs in GROUPS:
        part = lax.slice_in_dim(source, start * PAIR, (start + pairs) * PAIR, axis=2)
        low.append(lax.ppermute(part, order, onward))
        high.append(lax.ppermute(part, order, back))
        start += pairs
        source, _ = lax.optimization_barrier((key_value, part))
    normed, first_rows, last_rows = attention(queries, key_value, low, high, edge, conv_gain)

    before = lax.ppermute(last_rows, order, onward)
    after = lax.ppermute(first_rows, order, back)
    inner = inner_conv(normed, conv_kernel)

    local = w_in.shape[0]
    experts = local * time_count
    slots = max(2, 3 * frame_rows // (2 * experts))
    early = 2 * slots // 3
    sizes = (early, slots - early)
    served = jnp.where(overflow == 1, secondary, primary)
    place = jnp.where(
        slot < early,
        served * early + slot,
        experts * early + served * (slots - early) + slot - early,
    )
    mixed, *chunks = dispatch(
        normed, inner, before, after, conv_kernel, ffn_gain, place, [experts * c for c in sizes]
    )

    up = [(i, (i + 1) % group_count) for i in range(group_count)]
    down = [((i + 1) % group_count, i) for i in range(group_count)]
    add = lambda *vs: sum(v.astype(F32) for v in vs).astype(BF16)

    def arrive(chunk, size):
        sent = chunk.reshape(time_count, local * size, width)
        got = lax.all_to_all(sent, "tm", split_axis=0, concat_axis=0, tiled=True)
        return got.reshape(experts * size, width)

    def near(own):
        return lax.ppermute(own, "expert", up), lax.ppermute(own, "expert", down)

    def leave(summed, size):
        summed = summed.reshape(time_count, local * size, width)
        got = lax.all_to_all(summed, "tm", split_axis=0, concat_axis=0, tiled=True)
        return got.reshape(experts * size, width)

    after = lambda values, *others: lax.optimization_barrier((tuple(values), others))[0]
    across = [(i, (i + 2) % group_count) for i in range(group_count)]
    own_a = arrive(chunks[0], sizes[0])
    left_a, right_a = near(own_a)
    own_b = arrive(*after((chunks[1],), own_a), sizes[1])
    left_a, right_a = after((left_a, right_a), own_b)
    half = own_a.shape[0] // 2
    far_a = lax.ppermute(left_a[:half], "expert", up), lax.ppermute(right_a[half:], "expert", down)
    left_b, right_b = near(own_b)
    far_b = lax.ppermute(own_b, "expert", across)
    keep_a, go_up_a, go_down_a, up2_a, down2_a = ffn(own_a, left_a, right_a, far_a, w_in, w_out)
    below_a, above_a = lax.ppermute(go_up_a, "expert", up), lax.ppermute(go_down_a, "expert", down)
    (own_b,) = after((own_b,), keep_a)
    keep_b, to_right, to_left, to_far = ffn(own_b, left_b, right_b, (far_b,), w_in, w_out)
    below_a, above_a = after((below_a, above_a), keep_b)
    up2_a, down2_a = add(up2_a, below_a[0]), add(down2_a, above_a[0])
    up3_a, down3_a = lax.ppermute(up2_a, "expert", up), lax.ppermute(down2_a, "expert", down)
    to_right, to_left, to_far = after((to_right, to_left, to_far), up3_a, down3_a)
    parts_b = (
        lax.ppermute(to_right, "expert", up),
        lax.ppermute(to_left, "expert", down),
        lax.ppermute(to_far, "expert", across),
    )
    terms = (((0, 0), (1, 1), (3, None)), ((0, 1), (2, 1), (4, None)))
    total_a = home(terms, keep_a, above_a, below_a, up3_a, down3_a)
    back_a = leave(total_a, sizes[0])
    parts_b = after(parts_b, back_a)
    total_b = home([[(i, e) for i in range(4)] for e in range(2)], keep_b, *parts_b)
    back_b = leave(total_b, sizes[1])
    return combine(mixed, expert_gate, place, [back_a, back_b])


def solution(mesh):
    in_specs = (
        P(("tm", "expert"), None),
        P(None, ("tm", "expert"), None),
        P(),
        P(),
        P(),
        P(("tm", "expert")),
        P(("tm", "expert")),
        P(("tm", "expert")),
        P(("tm", "expert")),
        P(("tm", "expert")),
        P("tm", None, "expert"),
        P("tm", "expert", None),
    )
    out_specs = P(("tm", "expert"), None)
    return jax.shard_map(
        on_device, mesh=mesh, in_specs=in_specs, out_specs=out_specs, check_vma=False
    )
```

```python
import functools

import jax
import jax.numpy as jnp
from jax import lax
from jax.experimental import pallas as pl
from jax.experimental.pallas import tpu as pltpu
from jax.sharding import PartitionSpec as P

HEAD = 64
PAIR = 2 * HEAD
HALF = 256
TILE = 128
SPAN = 2 * HALF + TILE
EDGE = 16
GROUPS = (8, 4)
SIDE = 2
BLOCK = SIDE * PAIR
MIB = 1024 * 1024
STEP = 512
DEVICES = 32
F32 = jnp.float32
BF16 = jnp.bfloat16


def call(body, out_shape, cost, vmem, **kw):
    flops, moved = cost
    return pl.pallas_call(
        body,
        out_shape=out_shape,
        cost_estimate=pl.CostEstimate(flops=flops, bytes_accessed=moved, transcendentals=0),
        compiler_params=pltpu.CompilerParams(vmem_limit_bytes=vmem * MIB),
        **kw,
    )


def fill_bias(edge_ref, bias):
    @pl.when(pl.program_id(0) == 0)
    def _():
        row = lax.broadcasted_iota(jnp.int32, (TILE, SPAN), 0)
        col = lax.broadcasted_iota(jnp.int32, (TILE, SPAN), 1)
        for r in range(2):
            low = jnp.where(edge_ref[0] == 1, HALF - TILE * r, 0)
            high = jnp.where(edge_ref[1] == 1, 2 * HALF - TILE * r, SPAN)
            kept = (col > row) & (col - row < 2 * HALF) & (col >= low) & (col < high)
            bias[r] = jnp.where(kept, 0.0, -1e30)


def attend_pairs(q_ref, kv_ref, lo_ref, hi_ref, bias, put):
    lane = lax.broadcasted_iota(jnp.int32, (1, PAIR), 1)
    first = lane < HEAD
    only0 = jnp.where(first, 0.125, 0.0).astype(BF16)
    only1 = jnp.where(first, 0.0, 0.125).astype(BF16)
    ones = jnp.ones((SPAN, PAIR), BF16)
    for c in range(SIDE):
        cols = slice(c * PAIR, (c + 1) * PAIR)
        for r in range(2):
            if r == 0:
                join = lambda i: [lo_ref[i, :, cols], kv_ref[i, :, cols], hi_ref[i, :TILE, cols]]
            else:
                join = lambda i: [lo_ref[i, TILE:, cols], kv_ref[i, :, cols], hi_ref[i, :, cols]]
            rows = slice(r * TILE, (r + 1) * TILE)
            q = q_ref[rows, cols]
            both = jnp.concatenate([q * only0, q * only1], axis=0)
            s = lax.dot_general(
                both,
                jnp.concatenate(join(0), axis=0),
                (((1,), (1,)), ((), ())),
                preferred_element_type=F32,
            )
            s = s + jnp.concatenate([bias[r], bias[r]], axis=0)
            p = jnp.exp(s - jnp.max(s, axis=1, keepdims=True)).astype(BF16)
            values = jnp.concatenate([jnp.concatenate(join(1), axis=0), ones], axis=1)
            o = jnp.dot(p, values, preferred_element_type=F32)
            o = o[:, :PAIR] / o[:, PAIR:]
            put(c, rows, jnp.where(first, o[:TILE], o[TILE:]))


def attend_body(edge_ref, q_ref, kv_ref, lo_ref, hi_ref, out_ref, bias):
    fill_bias(edge_ref, bias)

    def put(c, rows, value):
        out_ref[rows, c * PAIR : (c + 1) * PAIR] = value

    attend_pairs(q_ref, kv_ref, lo_ref, hi_ref, bias, put)


def attend_norm_body(groups, edge_ref, q_ref, kv_ref, lo_ref, hi_ref, gain_ref, *rest):
    n = len(groups)
    earlier, (out_ref, low_ref, high_ref, bias, mine) = rest[:n], rest[n:]
    step = pl.program_id(0)
    fill_bias(edge_ref, bias)

    def put(c, rows, value):
        mine[step * SIDE + c, rows] = value

    attend_pairs(q_ref, kv_ref, lo_ref, hi_ref, bias, put)

    @pl.when(step == pl.num_programs(0) - 1)
    def _():
        blocks = [(ref, c) for ref, g in zip(earlier, groups) for c in range(g)]
        pieces = [(lambda ref=ref, c=c: ref[:, c * PAIR : (c + 1) * PAIR]) for ref, c in blocks]
        pieces += [(lambda c=c: mine[c]) for c in range(mine.shape[0])]
        total = jnp.zeros((2 * TILE, PAIR), F32)
        for piece in pieces:
            v = piece()
            total = total + v * v
        width = len(pieces) * PAIR
        scale = lax.rsqrt(jnp.sum(total, axis=1, keepdims=True) * (1.0 / width) + 1e-6)
        for c, piece in enumerate(pieces):
            cols = slice(c * PAIR, (c + 1) * PAIR)
            out_ref[:, cols] = (piece() * scale * gain_ref[:, cols]).astype(BF16)
        low_ref[...] = out_ref[:EDGE]
        high_ref[...] = out_ref[2 * TILE - EDGE :]


def attention(queries, key_value, low, high, edge, conv_gain):
    rows, width = queries.shape
    outs = []
    start = 0
    for g, pairs in enumerate(GROUPS):
        last = g == len(GROUPS) - 1
        base = [
            pl.BlockSpec(memory_space=pltpu.SMEM),
            pl.BlockSpec((rows, BLOCK), lambda j, s=start // SIDE: (0, s + j)),
            pl.BlockSpec((2, rows, BLOCK), lambda j, s=start // SIDE: (0, 0, s + j)),
            pl.BlockSpec((2, rows, BLOCK), lambda j: (0, 0, j)),
            pl.BlockSpec((2, rows, BLOCK), lambda j: (0, 0, j)),
        ]
        scratch = [pltpu.VMEM((2, TILE, SPAN), F32)]
        cost = (pairs * 16 * rows * SPAN * PAIR, pairs * 7 * rows * PAIR * 2)
        before, after = low[g], high[g]
        if outs:
            before, after, _ = lax.optimization_barrier((before, after, outs[-1]))
        args = (edge, queries, key_value, before, after)
        if not last:
            outs.append(
                call(
                    attend_body,
                    jax.ShapeDtypeStruct((rows, pairs * PAIR), F32),
                    cost,
                    58,
                    grid=(pairs // SIDE,),
                    in_specs=base,
                    out_specs=pl.BlockSpec((rows, BLOCK), lambda j: (0, j)),
                    scratch_shapes=scratch,
                )(*args)
            )
        else:
            whole = lambda *shape: pl.BlockSpec(shape, lambda j: (0,) * len(shape))
            return call(
                functools.partial(attend_norm_body, GROUPS[:-1]),
                [
                    jax.ShapeDtypeStruct((rows, width), BF16),
                    jax.ShapeDtypeStruct((EDGE, width), BF16),
                    jax.ShapeDtypeStruct((EDGE, width), BF16),
                ],
                cost,
                20,
                grid=(pairs // SIDE,),
                in_specs=base + [whole(1, width)] + [whole(*o.shape) for o in outs],
                out_specs=[whole(rows, width), whole(EDGE, width), whole(EDGE, width)],
                scratch_shapes=scratch + [pltpu.VMEM((pairs, rows, PAIR), F32)],
            )(*args, conv_gain[None], *outs)
        start += pairs


def silu(v):
    half = 0.5 * v
    return half + half * jnp.tanh(half)


def conv_rows(source, taps, first, count):
    total = jnp.zeros((count, PAIR), F32)
    for k in range(taps.shape[0]):
        total = total + taps[k : k + 1] * source[first + k : first + k + count]
    return source[first + 15 : first + 15 + count] + silu(total)


def inner_conv_body(normed_ref, taps_ref, out_ref, wide):
    wide[...] = normed_ref[...].astype(F32)
    count = 32
    for t in range(0, out_ref.shape[0], count):
        out_ref[t : t + count] = conv_rows(wide, taps_ref, EDGE + t - 15, count).astype(BF16)


def inner_conv(normed, taps):
    rows, width = normed.shape
    inner = rows - 2 * EDGE
    return call(
        inner_conv_body,
        jax.ShapeDtypeStruct((inner, width), BF16),
        (62 * inner * width * 64, 4 * rows * width),
        16,
        grid=(width // PAIR,),
        in_specs=[
            pl.BlockSpec((rows, PAIR), lambda j: (0, j)),
            pl.BlockSpec((taps.shape[0], PAIR), lambda j: (0, j)),
        ],
        out_specs=pl.BlockSpec((inner, PAIR), lambda j: (0, j)),
        scratch_shapes=[pltpu.VMEM((rows, PAIR), F32)],
    )(normed, taps)


def dispatch_body(normed_ref, inner_ref, low_ref, high_ref, taps_ref, gain_ref, place_ref, *rest):
    mixed_ref, outs, (wide,) = rest[0], rest[1:-1], rest[-1:]
    rows, width = normed_ref.shape
    for c in range(width // PAIR):
        cols = slice(c * PAIR, (c + 1) * PAIR)
        wide[0, :EDGE] = low_ref[:, cols].astype(F32)
        wide[0, EDGE:] = normed_ref[: 2 * EDGE, cols].astype(F32)
        wide[1, : 2 * EDGE] = normed_ref[rows - 2 * EDGE :, cols].astype(F32)
        wide[1, 2 * EDGE :] = high_ref[:, cols].astype(F32)
        taps = taps_ref.at[:, cols]
        mixed_ref[:EDGE, cols] = conv_rows(wide.at[0], taps, 1, EDGE).astype(BF16)
        mixed_ref[rows - EDGE :, cols] = conv_rows(wide.at[1], taps, 1, EDGE).astype(BF16)
    mixed_ref[EDGE : rows - EDGE] = inner_ref[...]
    mixed = mixed_ref[...].astype(F32)
    scale = lax.rsqrt(jnp.mean(mixed * mixed, axis=1, keepdims=True) + 1e-6)
    expert_in = (mixed * scale * gain_ref[...]).astype(BF16)
    first = 0
    for out_ref in outs:
        count = out_ref.shape[0]
        place = first + lax.broadcasted_iota(jnp.int32, (count, rows), 0)
        pick = jnp.where(place == place_ref[...], 1.0, 0.0).astype(BF16)
        out_ref[...] = jnp.dot(pick, expert_in, preferred_element_type=F32).astype(BF16)
        first += count


def dispatch(normed, inner, low, high, taps, gain, place, counts):
    rows, width = normed.shape
    return call(
        dispatch_body,
        [jax.ShapeDtypeStruct((rows, width), BF16)]
        + [jax.ShapeDtypeStruct((count, width), BF16) for count in counts],
        (2 * sum(counts) * rows * width, 8 * rows * width),
        24,
        scratch_shapes=[pltpu.VMEM((2, 3 * EDGE, PAIR), F32)],
    )(normed, inner, low, high, taps, gain[None], place[None])


def combine_body(mixed_ref, gate_ref, place_ref, *rest):
    parts, out_ref = rest[:-1], rest[-1]
    rows = mixed_ref.shape[0]
    total = None
    first = 0
    for part in parts:
        count = part.shape[0]
        place = first + lax.broadcasted_iota(jnp.int32, (rows, count), 1)
        pick = jnp.where(place == place_ref[...], 1.0, 0.0).astype(BF16)
        got = jnp.dot(pick, part[...], preferred_element_type=F32)
        total = got if total is None else total + got
        first += count
    out_ref[...] = (mixed_ref[...].astype(F32) + gate_ref[...] * total).astype(BF16)


def combine(mixed, gate, place, parts):
    rows, width = mixed.shape
    block = width // 2
    column = lambda n: pl.BlockSpec((n, block), lambda j: (0, j))
    fixed = pl.BlockSpec((rows, 1), lambda j: (0, 0))
    return call(
        combine_body,
        jax.ShapeDtypeStruct((rows, width), BF16),
        (2 * sum(p.shape[0] for p in parts) * rows * width, 8 * rows * width),
        16,
        grid=(width // block,),
        in_specs=[column(rows), fixed, fixed] + [column(p.shape[0]) for p in parts],
        out_specs=column(rows),
    )(mixed, gate[:, None], place[:, None], *parts)


def by_expert(n, axis):
    slots = n // DEVICES
    row = lax.broadcasted_iota(jnp.int32, (2 * n, 2 * n), axis)
    e = jnp.where(row >= n, 1, 0)
    r = row - e * n
    device = (r * (4096 // slots + 1)) >> 12
    place = device * slots + e * slots + r
    return jnp.where(place == lax.broadcasted_iota(jnp.int32, (2 * n, 2 * n), 1 - axis), 1.0, 0.0).astype(BF16)


def ffn_body(direct, own, left, right, *rest):
    far, (w_in, w_out, *rest) = (rest[:1], rest[1:]) if direct else (rest[:2], rest[2:])
    if direct:
        keep, to_right, to_left, to_far, *scratch = rest
    else:
        keep, up, down, up2, down2, *scratch = rest
    rows_in, hidden, first, second, sems = scratch
    n = own.shape[0] // 2
    width = own.shape[1]
    units = hidden.shape[1]
    step = STEP
    copies = {}
    for e in range(2):
        for which, (weight, held) in enumerate(((w_in, first), (w_out, second))):
            for t in range(weight.shape[2] // step):
                cols = slice(t * step, (t + 1) * step)
                copies[e, which, t] = pltpu.make_async_copy(
                    weight.at[e, :, cols], held.at[e, t], sems.at[e, which, t]
                )
                copies[e, which, t].start()
    order = by_expert(n, 0)
    for k, refs in enumerate(((own,), (left,), (right,), far)):
        block = jnp.concatenate([ref[...] for ref in refs], axis=0)
        block = jnp.dot(order, block, preferred_element_type=F32).astype(BF16)
        rows_in[0, k * n : (k + 1) * n] = block[:n]
        rows_in[1, k * n : (k + 1) * n] = block[n:]
    for e in range(2):
        for t in range(units // step):
            copies[e, 0, t].wait()
            part = jnp.dot(rows_in[e], first[e, t], preferred_element_type=F32)
            hidden[:, t * step : (t + 1) * step] = silu(part).astype(BF16)
        for t in range(width // step):
            copies[e, 1, t].wait()
            cols = slice(t * step, (t + 1) * step)
            part = jnp.dot(hidden[...], second[e, t], preferred_element_type=F32).astype(BF16)
            keep[e, :, cols] = part[:n]
            if direct:
                to_left[e, :, cols] = part[n : 2 * n]
                to_right[e, :, cols] = part[2 * n : 3 * n]
                to_far[e, :, cols] = part[3 * n :]
            elif e == 0:
                down[1, :, cols] = part[n : 2 * n]
                up2[:, cols] = part[2 * n : 3 * n]
                up[0, :, cols] = part[3 * n :]
            else:
                down2[:, cols] = part[n : 2 * n]
                up[1, :, cols] = part[2 * n : 3 * n]
                down[0, :, cols] = part[3 * n :]


def ffn(own, left, right, far, w_in, w_out):
    direct = len(far) == 1
    n = own.shape[0] // 2
    experts, width, units = w_in.shape
    pair = jax.ShapeDtypeStruct((2, n, width), BF16)
    single = jax.ShapeDtypeStruct((n, width), BF16)
    return call(
        functools.partial(ffn_body, direct),
        [pair] * 4 if direct else [pair, pair, pair, single, single],
        (experts * 4 * n * width * units * 4, 2 * experts * width * units * 2),
        42,
        in_specs=[
            *[pl.BlockSpec(memory_space=pltpu.VMEM)] * (3 + len(far)),
            pl.BlockSpec(memory_space=pl.ANY),
            pl.BlockSpec(memory_space=pl.ANY),
        ],
        scratch_shapes=[
            pltpu.VMEM((2, 4 * n, width), BF16),
            pltpu.VMEM((4 * n, units), BF16),
            pltpu.VMEM((2, units // STEP, width, STEP), BF16),
            pltpu.VMEM((2, width // STEP, units, STEP), BF16),
            pltpu.SemaphoreType.DMA((2, 2, max(units, width) // STEP)),
        ],
    )(own, left, right, *far, w_in, w_out)


def home_body(terms, *refs):
    ins, out_ref = refs[:-1], refs[-1]
    sums = []
    for chosen in terms:
        values = [(ins[i][...] if lead is None else ins[i][lead]).astype(F32) for i, lead in chosen]
        sums.append(sum(values[1:], values[0]).astype(BF16))
    rows = jnp.concatenate(sums, axis=0)
    order = by_expert(rows.shape[0] // 2, 1)
    out_ref[...] = jnp.dot(order, rows, preferred_element_type=F32).astype(BF16)


def home(terms, *arrays):
    _, n, width = arrays[0].shape
    return call(
        functools.partial(home_body, terms),
        jax.ShapeDtypeStruct((2 * n, width), BF16),
        (8 * n * n * width, 16 * n * width),
        24,
    )(*arrays)


def on_device(
    queries,
    key_value,
    conv_kernel,
    conv_gain,
    ffn_gain,
    expert_gate,
    primary,
    secondary,
    overflow,
    slot,
    w_in,
    w_out,
):
    frame_rows, width = queries.shape
    time_count = lax.axis_size("tm")
    group_count = lax.axis_size("expert")
    devices = time_count * group_count
    index = lax.axis_index("tm") * group_count + lax.axis_index("expert")
    edge = jnp.stack([index == 0, index == devices - 1]).astype(jnp.int32)
    order = ("tm", "expert")
    onward = [(i, i + 1) for i in range(devices - 1)]
    back = [(i + 1, i) for i in range(devices - 1)]

    low, high = [], []
    start = 0
    source = key_value
    for pairs in GROUPS:
        part = lax.slice_in_dim(source, start * PAIR, (start + pairs) * PAIR, axis=2)
        low.append(lax.ppermute(part, order, onward))
        high.append(lax.ppermute(part, order, back))
        start += pairs
        source, _ = lax.optimization_barrier((key_value, part))
    normed, first_rows, last_rows = attention(queries, key_value, low, high, edge, conv_gain)

    before = lax.ppermute(last_rows, order, onward)
    after = lax.ppermute(first_rows, order, back)
    inner = inner_conv(normed, conv_kernel)

    local = w_in.shape[0]
    experts = local * time_count
    slots = max(2, 3 * frame_rows // (2 * experts))
    early = slots // 3
    sizes = (early, slots - early)
    served = jnp.where(overflow == 1, secondary, primary)
    place = jnp.where(
        slot < early,
        served * early + slot,
        experts * early + served * (slots - early) + slot - early,
    )
    mixed, *chunks = dispatch(
        normed, inner, before, after, conv_kernel, ffn_gain, place, [experts * c for c in sizes]
    )

    up = [(i, (i + 1) % group_count) for i in range(group_count)]
    down = [((i + 1) % group_count, i) for i in range(group_count)]
    add = lambda *vs: sum(v.astype(F32) for v in vs).astype(BF16)

    def arrive(chunk, size):
        sent = chunk.reshape(time_count, local * size, width)
        got = lax.all_to_all(sent, "tm", split_axis=0, concat_axis=0, tiled=True)
        return got.reshape(experts * size, width)

    def near(own):
        return lax.ppermute(own, "expert", up), lax.ppermute(own, "expert", down)

    def leave(summed, size):
        summed = summed.reshape(time_count, local * size, width)
        got = lax.all_to_all(summed, "tm", split_axis=0, concat_axis=0, tiled=True)
        return got.reshape(experts * size, width)

    after = lambda values, *others: lax.optimization_barrier((tuple(values), others))[0]
    across = [(i, (i + 2) % group_count) for i in range(group_count)]
    own_a = arrive(chunks[0], sizes[0])
    left_a, right_a = near(own_a)
    far_a = lax.ppermute(own_a, "expert", across)
    own_b = arrive(*after((chunks[1],), own_a), sizes[1])
    left_b, right_b = near(own_b)
    left_a, right_a, far_a = after((left_a, right_a, far_a), own_b)
    keep_a, to_right, to_left, to_far = ffn(own_a, left_a, right_a, (far_a,), w_in, w_out)
    left_b, right_b = after((left_b, right_b), keep_a)
    half = own_b.shape[0] // 2
    far_b = lax.ppermute(left_b[:half], "expert", up), lax.ppermute(right_b[half:], "expert", down)
    to_right, to_left, to_far = after((to_right, to_left, to_far), *far_b)
    parts_a = (
        lax.ppermute(to_right, "expert", up),
        lax.ppermute(to_left, "expert", down),
        lax.ppermute(to_far, "expert", across),
    )
    keep_b, go_up, go_down, up2, down2 = ffn(own_b, left_b, right_b, far_b, w_in, w_out)
    parts_a = after(parts_a, keep_b)
    go_up, go_down = after((go_up, go_down), *parts_a)
    below, above = lax.ppermute(go_up, "expert", up), lax.ppermute(go_down, "expert", down)
    total_a = home([[(i, e) for i in range(4)] for e in range(2)], keep_a, *parts_a)
    back_a = leave(total_a, sizes[0])
    below, above = after((below, above), back_a)
    up2, down2 = add(up2, below[0]), add(down2, above[0])
    up3, down3 = lax.ppermute(up2, "expert", up), lax.ppermute(down2, "expert", down)
    terms = (((0, 0), (1, 1), (3, None)), ((0, 1), (2, 1), (4, None)))
    total_b = home(terms, keep_b, above, below, up3, down3)
    back_b = leave(total_b, sizes[1])
    return combine(mixed, expert_gate, place, [back_a, back_b])


def solution(mesh):
    in_specs = (
        P(("tm", "expert"), None),
        P(None, ("tm", "expert"), None),
        P(),
        P(),
        P(),
        P(("tm", "expert")),
        P(("tm", "expert")),
        P(("tm", "expert")),
        P(("tm", "expert")),
        P(("tm", "expert")),
        P("tm", None, "expert"),
        P("tm", "expert", None),
    )
    out_specs = P(("tm", "expert"), None)
    return jax.shard_map(
        on_device, mesh=mesh, in_specs=in_specs, out_specs=out_specs, check_vma=False
    )
```

```python
import functools

import jax
import jax.numpy as jnp
from jax import lax
from jax.experimental import pallas as pl
from jax.experimental.pallas import tpu as pltpu
from jax.sharding import PartitionSpec as P

HEAD = 64
PAIR = 2 * HEAD
HALF = 256
TILE = 128
SPAN = 2 * HALF + TILE
EDGE = 16
GROUPS = (8, 4)
SIDE = 2
BLOCK = SIDE * PAIR
MIB = 1024 * 1024
STEP = 512
DEVICES = 32
F32 = jnp.float32
BF16 = jnp.bfloat16


def call(body, out_shape, cost, vmem, **kw):
    flops, moved = cost
    return pl.pallas_call(
        body,
        out_shape=out_shape,
        cost_estimate=pl.CostEstimate(flops=flops, bytes_accessed=moved, transcendentals=0),
        compiler_params=pltpu.CompilerParams(vmem_limit_bytes=vmem * MIB),
        **kw,
    )


def fill_bias(edge_ref, bias):
    @pl.when(pl.program_id(0) == 0)
    def _():
        row = lax.broadcasted_iota(jnp.int32, (TILE, SPAN), 0)
        col = lax.broadcasted_iota(jnp.int32, (TILE, SPAN), 1)
        for r in range(2):
            low = jnp.where(edge_ref[0] == 1, HALF - TILE * r, 0)
            high = jnp.where(edge_ref[1] == 1, 2 * HALF - TILE * r, SPAN)
            kept = (col > row) & (col - row < 2 * HALF) & (col >= low) & (col < high)
            bias[r] = jnp.where(kept, 0.0, -1e30)


def attend_pairs(q_ref, kv_ref, lo_ref, hi_ref, bias, put):
    lane = lax.broadcasted_iota(jnp.int32, (1, PAIR), 1)
    first = lane < HEAD
    only0 = jnp.where(first, 0.125, 0.0).astype(BF16)
    only1 = jnp.where(first, 0.0, 0.125).astype(BF16)
    ones = jnp.ones((SPAN, PAIR), BF16)
    for c in range(SIDE):
        cols = slice(c * PAIR, (c + 1) * PAIR)
        for r in range(2):
            if r == 0:
                join = lambda i: [lo_ref[i, :, cols], kv_ref[i, :, cols], hi_ref[i, :TILE, cols]]
            else:
                join = lambda i: [lo_ref[i, TILE:, cols], kv_ref[i, :, cols], hi_ref[i, :, cols]]
            rows = slice(r * TILE, (r + 1) * TILE)
            q = q_ref[rows, cols]
            both = jnp.concatenate([q * only0, q * only1], axis=0)
            s = lax.dot_general(
                both,
                jnp.concatenate(join(0), axis=0),
                (((1,), (1,)), ((), ())),
                preferred_element_type=F32,
            )
            s = s + jnp.concatenate([bias[r], bias[r]], axis=0)
            p = jnp.exp(s - jnp.max(s, axis=1, keepdims=True)).astype(BF16)
            values = jnp.concatenate([jnp.concatenate(join(1), axis=0), ones], axis=1)
            o = jnp.dot(p, values, preferred_element_type=F32)
            o = o[:, :PAIR] / o[:, PAIR:]
            put(c, rows, jnp.where(first, o[:TILE], o[TILE:]))


def attend_body(edge_ref, q_ref, kv_ref, lo_ref, hi_ref, out_ref, bias):
    fill_bias(edge_ref, bias)

    def put(c, rows, value):
        out_ref[rows, c * PAIR : (c + 1) * PAIR] = value

    attend_pairs(q_ref, kv_ref, lo_ref, hi_ref, bias, put)


def attend_norm_body(groups, edge_ref, q_ref, kv_ref, lo_ref, hi_ref, gain_ref, *rest):
    n = len(groups)
    earlier, (out_ref, low_ref, high_ref, bias, mine) = rest[:n], rest[n:]
    step = pl.program_id(0)
    fill_bias(edge_ref, bias)

    def put(c, rows, value):
        mine[step * SIDE + c, rows] = value

    attend_pairs(q_ref, kv_ref, lo_ref, hi_ref, bias, put)

    @pl.when(step == pl.num_programs(0) - 1)
    def _():
        blocks = [(ref, c) for ref, g in zip(earlier, groups) for c in range(g)]
        pieces = [(lambda ref=ref, c=c: ref[:, c * PAIR : (c + 1) * PAIR]) for ref, c in blocks]
        pieces += [(lambda c=c: mine[c]) for c in range(mine.shape[0])]
        total = jnp.zeros((2 * TILE, PAIR), F32)
        for piece in pieces:
            v = piece()
            total = total + v * v
        width = len(pieces) * PAIR
        scale = lax.rsqrt(jnp.sum(total, axis=1, keepdims=True) * (1.0 / width) + 1e-6)
        for c, piece in enumerate(pieces):
            cols = slice(c * PAIR, (c + 1) * PAIR)
            out_ref[:, cols] = (piece() * scale * gain_ref[:, cols]).astype(BF16)
        low_ref[...] = out_ref[:EDGE]
        high_ref[...] = out_ref[2 * TILE - EDGE :]


def attention(queries, key_value, low, high, edge, conv_gain):
    rows, width = queries.shape
    outs = []
    start = 0
    for g, pairs in enumerate(GROUPS):
        last = g == len(GROUPS) - 1
        base = [
            pl.BlockSpec(memory_space=pltpu.SMEM),
            pl.BlockSpec((rows, BLOCK), lambda j, s=start // SIDE: (0, s + j)),
            pl.BlockSpec((2, rows, BLOCK), lambda j, s=start // SIDE: (0, 0, s + j)),
            pl.BlockSpec((2, rows, BLOCK), lambda j: (0, 0, j)),
            pl.BlockSpec((2, rows, BLOCK), lambda j: (0, 0, j)),
        ]
        scratch = [pltpu.VMEM((2, TILE, SPAN), F32)]
        cost = (pairs * 16 * rows * SPAN * PAIR, pairs * 7 * rows * PAIR * 2)
        before, after = low[g], high[g]
        if outs:
            before, after, _ = lax.optimization_barrier((before, after, outs[-1]))
        args = (edge, queries, key_value, before, after)
        if not last:
            outs.append(
                call(
                    attend_body,
                    jax.ShapeDtypeStruct((rows, pairs * PAIR), F32),
                    cost,
                    58,
                    grid=(pairs // SIDE,),
                    in_specs=base,
                    out_specs=pl.BlockSpec((rows, BLOCK), lambda j: (0, j)),
                    scratch_shapes=scratch,
                )(*args)
            )
        else:
            whole = lambda *shape: pl.BlockSpec(shape, lambda j: (0,) * len(shape))
            return call(
                functools.partial(attend_norm_body, GROUPS[:-1]),
                [
                    jax.ShapeDtypeStruct((rows, width), BF16),
                    jax.ShapeDtypeStruct((EDGE, width), BF16),
                    jax.ShapeDtypeStruct((EDGE, width), BF16),
                ],
                cost,
                20,
                grid=(pairs // SIDE,),
                in_specs=base + [whole(1, width)] + [whole(*o.shape) for o in outs],
                out_specs=[whole(rows, width), whole(EDGE, width), whole(EDGE, width)],
                scratch_shapes=scratch + [pltpu.VMEM((pairs, rows, PAIR), F32)],
            )(*args, conv_gain[None], *outs)
        start += pairs


def silu(v):
    half = 0.5 * v
    return half + half * jnp.tanh(half)


def conv_rows(source, taps, first, count):
    total = jnp.zeros((count, PAIR), F32)
    for k in range(taps.shape[0]):
        total = total + taps[k : k + 1] * source[first + k : first + k + count]
    return source[first + 15 : first + 15 + count] + silu(total)


def inner_conv_body(normed_ref, taps_ref, out_ref, wide):
    wide[...] = normed_ref[...].astype(F32)
    count = 32
    for t in range(0, out_ref.shape[0], count):
        out_ref[t : t + count] = conv_rows(wide, taps_ref, EDGE + t - 15, count).astype(BF16)


def inner_conv(normed, taps):
    rows, width = normed.shape
    inner = rows - 2 * EDGE
    return call(
        inner_conv_body,
        jax.ShapeDtypeStruct((inner, width), BF16),
        (62 * inner * width * 64, 4 * rows * width),
        16,
        grid=(width // PAIR,),
        in_specs=[
            pl.BlockSpec((rows, PAIR), lambda j: (0, j)),
            pl.BlockSpec((taps.shape[0], PAIR), lambda j: (0, j)),
        ],
        out_specs=pl.BlockSpec((inner, PAIR), lambda j: (0, j)),
        scratch_shapes=[pltpu.VMEM((rows, PAIR), F32)],
    )(normed, taps)


def dispatch_body(normed_ref, inner_ref, low_ref, high_ref, taps_ref, gain_ref, place_ref, *rest):
    mixed_ref, outs, (wide,) = rest[0], rest[1:-1], rest[-1:]
    rows, width = normed_ref.shape
    for c in range(width // PAIR):
        cols = slice(c * PAIR, (c + 1) * PAIR)
        wide[0, :EDGE] = low_ref[:, cols].astype(F32)
        wide[0, EDGE:] = normed_ref[: 2 * EDGE, cols].astype(F32)
        wide[1, : 2 * EDGE] = normed_ref[rows - 2 * EDGE :, cols].astype(F32)
        wide[1, 2 * EDGE :] = high_ref[:, cols].astype(F32)
        taps = taps_ref.at[:, cols]
        mixed_ref[:EDGE, cols] = conv_rows(wide.at[0], taps, 1, EDGE).astype(BF16)
        mixed_ref[rows - EDGE :, cols] = conv_rows(wide.at[1], taps, 1, EDGE).astype(BF16)
    mixed_ref[EDGE : rows - EDGE] = inner_ref[...]
    mixed = mixed_ref[...].astype(F32)
    scale = lax.rsqrt(jnp.mean(mixed * mixed, axis=1, keepdims=True) + 1e-6)
    expert_in = (mixed * scale * gain_ref[...]).astype(BF16)
    first = 0
    for out_ref in outs:
        count = out_ref.shape[0]
        place = first + lax.broadcasted_iota(jnp.int32, (count, rows), 0)
        pick = jnp.where(place == place_ref[...], 1.0, 0.0).astype(BF16)
        out_ref[...] = jnp.dot(pick, expert_in, preferred_element_type=F32).astype(BF16)
        first += count


def dispatch(normed, inner, low, high, taps, gain, place, counts):
    rows, width = normed.shape
    return call(
        dispatch_body,
        [jax.ShapeDtypeStruct((rows, width), BF16)]
        + [jax.ShapeDtypeStruct((count, width), BF16) for count in counts],
        (2 * sum(counts) * rows * width, 8 * rows * width),
        24,
        scratch_shapes=[pltpu.VMEM((2, 3 * EDGE, PAIR), F32)],
    )(normed, inner, low, high, taps, gain[None], place[None])


def combine_body(mixed_ref, gate_ref, place_ref, *rest):
    parts, out_ref = rest[:-1], rest[-1]
    rows = mixed_ref.shape[0]
    total = None
    first = 0
    for part in parts:
        count = part.shape[0]
        place = first + lax.broadcasted_iota(jnp.int32, (rows, count), 1)
        pick = jnp.where(place == place_ref[...], 1.0, 0.0).astype(BF16)
        got = jnp.dot(pick, part[...], preferred_element_type=F32)
        total = got if total is None else total + got
        first += count
    out_ref[...] = (mixed_ref[...].astype(F32) + gate_ref[...] * total).astype(BF16)


def combine(mixed, gate, place, parts):
    rows, width = mixed.shape
    block = width // 2
    column = lambda n: pl.BlockSpec((n, block), lambda j: (0, j))
    fixed = pl.BlockSpec((rows, 1), lambda j: (0, 0))
    return call(
        combine_body,
        jax.ShapeDtypeStruct((rows, width), BF16),
        (2 * sum(p.shape[0] for p in parts) * rows * width, 8 * rows * width),
        16,
        grid=(width // block,),
        in_specs=[column(rows), fixed, fixed] + [column(p.shape[0]) for p in parts],
        out_specs=column(rows),
    )(mixed, gate[:, None], place[:, None], *parts)


def by_expert(n, axis):
    slots = n // DEVICES
    row = lax.broadcasted_iota(jnp.int32, (2 * n, 2 * n), axis)
    e = jnp.where(row >= n, 1, 0)
    r = row - e * n
    device = (r * (4096 // slots + 1)) >> 12
    place = device * slots + e * slots + r
    return jnp.where(place == lax.broadcasted_iota(jnp.int32, (2 * n, 2 * n), 1 - axis), 1.0, 0.0).astype(BF16)


def ffn_body(direct, own, left, right, *rest):
    far, (w_in, w_out, *rest) = (rest[:1], rest[1:]) if direct else (rest[:2], rest[2:])
    if direct:
        keep, to_right, to_left, to_far, *scratch = rest
    else:
        keep, up, down, up2, down2, *scratch = rest
    rows_in, hidden, first, second, sems = scratch
    n = own.shape[0] // 2
    width = own.shape[1]
    units = hidden.shape[1]
    step = STEP
    copies = {}
    for e in range(2):
        for which, (weight, held) in enumerate(((w_in, first), (w_out, second))):
            for t in range(weight.shape[2] // step):
                cols = slice(t * step, (t + 1) * step)
                copies[e, which, t] = pltpu.make_async_copy(
                    weight.at[e, :, cols], held.at[e, t], sems.at[e, which, t]
                )
                copies[e, which, t].start()
    order = by_expert(n, 0)
    for k, refs in enumerate(((own,), (left,), (right,), far)):
        block = jnp.concatenate([ref[...] for ref in refs], axis=0)
        block = jnp.dot(order, block, preferred_element_type=F32).astype(BF16)
        rows_in[0, k * n : (k + 1) * n] = block[:n]
        rows_in[1, k * n : (k + 1) * n] = block[n:]
    for e in range(2):
        for t in range(units // step):
            copies[e, 0, t].wait()
            part = jnp.dot(rows_in[e], first[e, t], preferred_element_type=F32)
            hidden[:, t * step : (t + 1) * step] = silu(part).astype(BF16)
        for t in range(width // step):
            copies[e, 1, t].wait()
            cols = slice(t * step, (t + 1) * step)
            part = jnp.dot(hidden[...], second[e, t], preferred_element_type=F32).astype(BF16)
            keep[e, :, cols] = part[:n]
            if direct:
                to_left[e, :, cols] = part[n : 2 * n]
                to_right[e, :, cols] = part[2 * n : 3 * n]
                to_far[e, :, cols] = part[3 * n :]
            elif e == 0:
                down[1, :, cols] = part[n : 2 * n]
                up2[:, cols] = part[2 * n : 3 * n]
                up[0, :, cols] = part[3 * n :]
            else:
                down2[:, cols] = part[n : 2 * n]
                up[1, :, cols] = part[2 * n : 3 * n]
                down[0, :, cols] = part[3 * n :]


def ffn(own, left, right, far, w_in, w_out):
    direct = len(far) == 1
    n = own.shape[0] // 2
    experts, width, units = w_in.shape
    pair = jax.ShapeDtypeStruct((2, n, width), BF16)
    single = jax.ShapeDtypeStruct((n, width), BF16)
    return call(
        functools.partial(ffn_body, direct),
        [pair] * 4 if direct else [pair, pair, pair, single, single],
        (experts * 4 * n * width * units * 4, 2 * experts * width * units * 2),
        42,
        in_specs=[
            *[pl.BlockSpec(memory_space=pltpu.VMEM)] * (3 + len(far)),
            pl.BlockSpec(memory_space=pl.ANY),
            pl.BlockSpec(memory_space=pl.ANY),
        ],
        scratch_shapes=[
            pltpu.VMEM((2, 4 * n, width), BF16),
            pltpu.VMEM((4 * n, units), BF16),
            pltpu.VMEM((2, units // STEP, width, STEP), BF16),
            pltpu.VMEM((2, width // STEP, units, STEP), BF16),
            pltpu.SemaphoreType.DMA((2, 2, max(units, width) // STEP)),
        ],
    )(own, left, right, *far, w_in, w_out)


def home_body(terms, *refs):
    ins, out_ref = refs[:-1], refs[-1]
    sums = []
    for chosen in terms:
        values = [(ins[i][...] if lead is None else ins[i][lead]).astype(F32) for i, lead in chosen]
        sums.append(sum(values[1:], values[0]).astype(BF16))
    rows = jnp.concatenate(sums, axis=0)
    order = by_expert(rows.shape[0] // 2, 1)
    out_ref[...] = jnp.dot(order, rows, preferred_element_type=F32).astype(BF16)


def home(terms, *arrays):
    _, n, width = arrays[0].shape
    return call(
        functools.partial(home_body, terms),
        jax.ShapeDtypeStruct((2 * n, width), BF16),
        (8 * n * n * width, 16 * n * width),
        24,
    )(*arrays)


def on_device(
    queries,
    key_value,
    conv_kernel,
    conv_gain,
    ffn_gain,
    expert_gate,
    primary,
    secondary,
    overflow,
    slot,
    w_in,
    w_out,
):
    frame_rows, width = queries.shape
    time_count = lax.axis_size("tm")
    group_count = lax.axis_size("expert")
    devices = time_count * group_count
    index = lax.axis_index("tm") * group_count + lax.axis_index("expert")
    edge = jnp.stack([index == 0, index == devices - 1]).astype(jnp.int32)
    order = ("tm", "expert")
    onward = [(i, i + 1) for i in range(devices - 1)]
    back = [(i + 1, i) for i in range(devices - 1)]

    low, high = [], []
    start = 0
    source = key_value
    for pairs in GROUPS:
        part = lax.slice_in_dim(source, start * PAIR, (start + pairs) * PAIR, axis=2)
        low.append(lax.ppermute(part, order, onward))
        high.append(lax.ppermute(part, order, back))
        start += pairs
        source, _ = lax.optimization_barrier((key_value, part))
    normed, first_rows, last_rows = attention(queries, key_value, low, high, edge, conv_gain)

    before = lax.ppermute(last_rows, order, onward)
    after = lax.ppermute(first_rows, order, back)
    inner = inner_conv(normed, conv_kernel)

    local = w_in.shape[0]
    experts = local * time_count
    slots = max(2, 3 * frame_rows // (2 * experts))
    early = 2 * slots // 3
    sizes = (early, slots - early)
    served = jnp.where(overflow == 1, secondary, primary)
    place = jnp.where(
        slot < early,
        served * early + slot,
        experts * early + served * (slots - early) + slot - early,
    )
    mixed, *chunks = dispatch(
        normed, inner, before, after, conv_kernel, ffn_gain, place, [experts * c for c in sizes]
    )

    up = [(i, (i + 1) % group_count) for i in range(group_count)]
    down = [((i + 1) % group_count, i) for i in range(group_count)]
    add = lambda *vs: sum(v.astype(F32) for v in vs).astype(BF16)

    def arrive(chunk, size):
        sent = chunk.reshape(time_count, local * size, width)
        got = lax.all_to_all(sent, "tm", split_axis=0, concat_axis=0, tiled=True)
        return got.reshape(experts * size, width)

    def near(own):
        return lax.ppermute(own, "expert", up), lax.ppermute(own, "expert", down)

    def leave(summed, size):
        summed = summed.reshape(time_count, local * size, width)
        got = lax.all_to_all(summed, "tm", split_axis=0, concat_axis=0, tiled=True)
        return got.reshape(experts * size, width)

    after = lambda values, *others: lax.optimization_barrier((tuple(values), others))[0]
    across = [(i, (i + 2) % group_count) for i in range(group_count)]
    own_a = arrive(chunks[0], sizes[0])
    left_a, right_a = near(own_a)
    own_b = arrive(*after((chunks[1],), own_a), sizes[1])
    left_a, right_a = after((left_a, right_a), own_b)
    half = own_a.shape[0] // 2
    far_a = lax.ppermute(left_a[:half], "expert", up), lax.ppermute(right_a[half:], "expert", down)
    left_b, right_b = near(own_b)
    far_b = lax.ppermute(own_b, "expert", across)
    keep_a, go_up_a, go_down_a, up2_a, down2_a = ffn(own_a, left_a, right_a, far_a, w_in, w_out)
    below_a, above_a = lax.ppermute(go_up_a, "expert", up), lax.ppermute(go_down_a, "expert", down)
    (own_b,) = after((own_b,), keep_a)
    keep_b, to_right, to_left, to_far = ffn(own_b, left_b, right_b, (far_b,), w_in, w_out)
    below_a, above_a = after((below_a, above_a), keep_b)
    up2_a, down2_a = add(up2_a, below_a[0]), add(down2_a, above_a[0])
    up3_a, down3_a = lax.ppermute(up2_a, "expert", up), lax.ppermute(down2_a, "expert", down)
    to_right, to_left, to_far = after((to_right, to_left, to_far), up3_a, down3_a)
    parts_b = (
        lax.ppermute(to_right, "expert", up),
        lax.ppermute(to_left, "expert", down),
        lax.ppermute(to_far, "expert", across),
    )
    terms = (((0, 0), (1, 1), (3, None)), ((0, 1), (2, 1), (4, None)))
    total_a = home(terms, keep_a, above_a, below_a, up3_a, down3_a)
    back_a = leave(total_a, sizes[0])
    parts_b = after(parts_b, back_a)
    total_b = home([[(i, e) for i in range(4)] for e in range(2)], keep_b, *parts_b)
    back_b = leave(total_b, sizes[1])
    return combine(mixed, expert_gate, place, [back_a, back_b])


def solution(mesh):
    in_specs = (
        P(("tm", "expert"), None),
        P(None, ("tm", "expert"), None),
        P(),
        P(),
        P(),
        P(("tm", "expert")),
        P(("tm", "expert")),
        P(("tm", "expert")),
        P(("tm", "expert")),
        P(("tm", "expert")),
        P("tm", None, "expert"),
        P("tm", "expert", None),
    )
    out_specs = P(("tm", "expert"), None)
    return jax.shard_map(
        on_device, mesh=mesh, in_specs=in_specs, out_specs=out_specs, check_vma=False
    )
```
